256 devices in a mesh: psi: 8 (over z), theta: 32 (over y, x, core).
Axes of the slice: x: 4, y: 4, z: 8, core: 2. Of those that a mesh axis runs over, the one named last changes fastest.
Arguments:
- sample_values: float32 [262144], P('theta'), may hold values from -6 to 6
- sample_coords: float32 [3, 262144], P(None, 'theta'), may hold values from 0 to 0.999
- tile_ids: int32 [262144, 1], P('theta'), may hold values from 0 to 31; in each aligned block of 8192 rows (0 to 8191, 8192 to 16383, ...) at most 512 rows name the same one
- phi_pixels: int32 [262144], P('theta'), may hold values from 0 to 2303
- wigner_table: bfloat16 [1152, 16, 32, 1152], P('theta', 'psi'), may hold values from -1 to 1
- beam: float32 [16, 1152], P('psi'), may hold values from -6 to 6
Outputs:
- sky: float32 [2, 1152, 1152], P(None, 'theta', 'psi')
The draws below stay inside these ranges and needn't reach their ends.
Inputs may be any that keep to these rules, and one draw needn't show every extreme that they name: `tile_ids`: at most 512 of the samples of one device name the same cycle.
All inputs are finite; a program needn't handle non-finite values.
Results may differ from the reference program's by a relative error of at most 0.006.
Values may be sent and summed in bfloat16 or wider, within the bound.
No kernel may reach another device: no remote copies, remote signals or barrier semaphores. Data moves between devices by JAX's collectives and lax.ppermute only.
A program may use at most 128 MiB of HBM per device.

```python
import math
import jax
import jax.numpy as jnp
import numpy as np
from jax import lax

S_DEV = 8192
M_DEV = 36
M = 1152
L = 1152
NPHI = 2304
PSI = 16
NTH = 32
CAP = 512
SAMPLES = 262144
N_THETA = 32


def place_ends(result, rng, low, high):
    index_at = [jax.random.randint(jax.random.fold_in(rng, axis), (), 0, length) for axis, length in enumerate(result.shape)]
    widest = result.shape.index(max(result.shape))
    neighbour = index_at[:widest] + [(index_at[widest] + 1) % result.shape[widest]] + index_at[widest + 1:]
    return result.at[tuple(index_at)].set(low).at[tuple(neighbour)].set(high)


def block_scale(key, shape, pieces, low, top_value):
    factor_of, own = 1.0, jax.random.fold_in(key, 6)
    for dim, parts in pieces:
        steps = jnp.exp(jax.random.uniform(jax.random.fold_in(own, dim), (parts,), jnp.float32, low / len(pieces), top_value / len(pieces)))
        factor_of = factor_of * jnp.repeat(steps, shape[dim] // parts).reshape([-1 if axis == dim else 1 for axis in range(len(shape))])
    return factor_of


def deal_out(stream_key, own, number, rows, number_of, top, most, lean):
    order = jax.random.permutation(stream_key, number_of)
    heavy_load, usual = shares(number_of, rows * top, most, lean, True), shares(number_of, rows * top, most, lean, False)
    places = jnp.arange(number_of)

    def named(lengths, rotation):
        used = int((lengths > 0).sum())
        fixed = max(1, used // 4)
        moved = fixed + (places - fixed + rotation * (used - fixed)) % max(1, number_of - fixed)
        return jnp.zeros((number_of,), jnp.int32).at[order[jnp.where(places < fixed, places, moved)]].set(jnp.asarray(lengths, jnp.int32))

    lengths = jnp.where(number % 4 == 0, named(heavy_load, number // 4), named(usual, number - number // 4 - 1))
    mixed = jax.random.permutation(jax.random.fold_in(own, 3), number_of)
    donor, receiver = mixed[0:number_of // 2 * 2:2], mixed[1:number_of // 2 * 2:2]
    slack = jnp.minimum(lengths[donor] - 1, most - lengths[receiver]) // 2
    slack = jnp.where((donor == order[0]) | (receiver == order[0]) | (lengths[receiver] == 0), 0, jnp.maximum(slack, 0))
    moved = jax.random.randint(jax.random.fold_in(own, 4), (number_of // 2,), 0, 1 << 20) % (slack + 1)
    lengths = lengths.at[donor].add(-moved).at[receiver].add(moved)
    items = jnp.searchsorted(jnp.cumsum(lengths), jnp.arange(rows * top), side="right").astype(jnp.int32)
    table = items.reshape(top, rows).T
    table = table[jax.random.permutation(jax.random.fold_in(own, 1), rows)]
    rotation = jax.random.randint(jax.random.fold_in(own, 2), (rows, 1), 0, top)
    return jnp.take_along_axis(table, (jnp.arange(top)[None, :] + rotation) % top, axis=1)


def shares(number_of, total, limit, lean, full):
    weights = [(1 << 20) // math.isqrt(grade ** lean) + 1 for grade in range(1, number_of + 1)]
    largest = limit if full else min(limit, max(-(-total // number_of), total * weights[0] // sum(weights)))
    least = 1 if total - largest >= number_of - 1 else 0
    counts, surplus = [largest] + [least] * (number_of - 1), total - largest - least * (number_of - 1)
    while surplus > 0:
        free = [i for i in range(1, number_of) if counts[i] < largest] or [i for i in range(1, number_of) if counts[i] < limit]
        mass, budget = sum([weights[i] for i in free]), surplus
        for i in free:
            addition = min(limit - counts[i], max(1, budget * weights[i] // mass), surplus)
            counts[i] = counts[i] + addition
            surplus = surplus - addition
    return np.array(counts)


def scatter_about(key, dims, deviation, reach, shards=(), held_as=jnp.bfloat16):
    factor_of = block_scale(key, dims, shards, -0.22, 0.18) if shards else 1.0
    result = jax.random.normal(key, dims, jnp.float32) * deviation * factor_of
    return jnp.minimum(jnp.maximum(result, -reach), reach).astype(held_as)


def setup_inputs(seed: int = 0) -> dict:
    key_of = jax.random.split(jax.random.key(seed), 7)
    sample_values = scatter_about(key_of[0], (SAMPLES,), 1.0, 6.0, ((0, 32),), jnp.float32)
    sample_coords = jnp.clip(0.999 * jax.random.uniform(key_of[1], (3, SAMPLES), jnp.float32) ** block_scale(key_of[1], (3, SAMPLES), ((1, 32),), -0.2, 0.2), 0.0, 0.999)
    tile_ids_keys = jax.random.split(jax.random.fold_in(key_of[2], 1), SAMPLES // S_DEV)
    tile_ids_turns = jax.random.permutation(jax.random.fold_in(key_of[2], 3), SAMPLES // S_DEV)
    tile_ids = jax.vmap(lambda own, number: deal_out(jax.random.fold_in(key_of[2], 2), own, number, S_DEV, N_THETA, 1, CAP, 2))(tile_ids_keys, tile_ids_turns).reshape((SAMPLES, 1))
    phi_pixels = place_ends(jax.random.randint(key_of[3], (SAMPLES,), 0, NPHI), jax.random.fold_in(key_of[3], 1), 0, NPHI - 1).astype(jnp.int32)
    wigner_table = scatter_about(key_of[4], (M, PSI, NTH, L), NTH ** -0.5, 1.0, ((0, 32), (1, 8)))
    beam = scatter_about(key_of[5], (PSI, L), 1.0, 6.0, ((0, 8),), jnp.float32)
    return {"sample_values": sample_values, "sample_coords": sample_coords, "tile_ids": tile_ids, "phi_pixels": phi_pixels, "wigner_table": wigner_table, "beam": beam}


two_pi = 2.0 * math.pi

def phi_kernel(offset):
    inner = 1.0 - 0.25 * offset * offset
    return jnp.where(jnp.abs(offset) < 2.0, inner * inner, 0.0)

def psi_weights(sample_angle, plane_angle, plane_count):
    separation = sample_angle[None, :] - plane_angle[:, None]
    nyquist = plane_count // 2
    running = jnp.ones_like(separation)
    for harmonic in range(1, nyquist):
        running = running + 2.0 * jnp.cos(harmonic * separation)
    running = running + jnp.cos(nyquist * separation)
    return running / plane_count

def psi_basis(channels, planes, plane_count):
    harmonic = (channels + 1) // 2
    phase_angle = two_pi * (harmonic[:, None] * planes[None, :] % plane_count).astype(jnp.float32) / plane_count
    basis_rows = jnp.where((channels % 2 == 1)[:, None], jnp.cos(phase_angle), jnp.sin(phase_angle))
    factor = jnp.where((channels == plane_count - 1)[:, None], 1.0, 2.0)
    return jnp.where((channels == 0)[:, None], 1.0, basis_rows * factor)

def fourier_table(nphi):
    pixel_ids = jnp.arange(nphi, dtype=jnp.int32)
    wave_ids = jnp.arange(nphi // 2, dtype=jnp.int32)
    phase_angle = two_pi * (pixel_ids[:, None] * wave_ids[None, :] % nphi).astype(jnp.float32) / nphi
    return jnp.concatenate([jnp.cos(phase_angle), -jnp.sin(phase_angle)], axis=1).astype(jnp.bfloat16)

def reference(sample_values, sample_coords, tile_ids, phi_pixels, wigner_table, beam):
    planes = jnp.arange(PSI, dtype=jnp.int32)
    plane_angle = two_pi * planes.astype(jnp.float32) / PSI
    amplitude = sample_values[None, :] * psi_weights(two_pi * sample_coords[2], plane_angle, PSI)
    cycle_frac = sample_coords[0]
    pixel_frac = sample_coords[1]
    cycle_ids = tile_ids[:, 0]
    sphere_cube = jnp.zeros((NTH + 1, PSI, NPHI), jnp.float32)
    for cycle_step, cycle_weight in ((0, 1.0 - cycle_frac), (1, cycle_frac)):
        left_rows = (cycle_weight[None, :] * amplitude).astype(jnp.bfloat16)
        left_rows = lax.optimization_barrier(left_rows).astype(jnp.float32)
        for pixel_step in (-1, 0, 1, 2):
            weight = phi_kernel(pixel_step - pixel_frac).astype(jnp.bfloat16)
            weight = lax.optimization_barrier(weight).astype(jnp.float32)
            column = (phi_pixels + pixel_step) % NPHI
            sphere_cube = sphere_cube.at[cycle_ids + cycle_step, :, column].add((left_rows * weight[None, :]).T)
    sphere_cube = sphere_cube[:NTH]
    basis_rows = psi_basis(planes, planes, PSI)
    coeffs = jnp.einsum('cp,rpq->crq', basis_rows, sphere_cube, precision=lax.Precision.HIGHEST).astype(jnp.bfloat16)
    table = fourier_table(NPHI)
    flat_rows = coeffs.reshape(PSI * NTH, NPHI)
    norm_scale = 1.0 / math.sqrt(NPHI)
    spectrum = jnp.dot(flat_rows, table, preferred_element_type=jnp.float32) * norm_scale
    freq = jnp.moveaxis(spectrum.astype(jnp.bfloat16).reshape(PSI, NTH, 2, M), 2, 0)
    table_blocks = wigner_table.reshape(N_THETA, M_DEV, PSI, NTH, L)
    freq_blocks = jnp.moveaxis(freq.reshape(2, PSI, NTH, N_THETA, M_DEV), 3, 0)
    beam_scale = 1.0 / math.sqrt(PSI)

    def one_block(block_item):
        table_part, freq_part = block_item
        projected = jnp.einsum('mcrl,kcrm->kcml', table_part.astype(jnp.float32), freq_part.astype(jnp.float32), precision=lax.Precision.HIGHEST)
        return jnp.einsum('cl,kcml->kml', beam, projected, precision=lax.Precision.HIGHEST) * beam_scale
    sky_blocks = lax.map(one_block, (table_blocks, freq_blocks))
    return jnp.moveaxis(sky_blocks, 0, 1).reshape(2, M, L)
```

```python
import math

import jax
import jax.numpy as jnp
import numpy as np
from jax import lax
from jax.experimental import pallas as pl
from jax.experimental.pallas import tpu as pltpu
from jax.sharding import PartitionSpec as P

LANES = 128
STRIDE = 253
BLOCK = 256
NT = (((1,), (1,)), ((), ()))


def fourier_rows(nphi, blocks):
    pixel = (STRIDE * np.arange(blocks)[:, None] + np.arange(BLOCK)[None, :] - 1) % nphi
    waves = np.arange(nphi // 2)
    phase = (2.0 * math.pi / nphi) * (waves[:, None] * pixel.reshape(1, -1) % nphi)
    return np.stack([np.cos(phase), -np.sin(phase)]).astype(jnp.bfloat16)


def deposit_kernel(
    blocks, cycles, nphi, nyquist, psi_ref, v_ref, coords_ref, t_ref, o_ref, table_hbm, out_ref,
    fields, ids, left, right, cube, table, sem,
):
    copy = pltpu.make_async_copy(table_hbm, table, sem)
    copy.start()
    rows = v_ref.shape[0]
    for i in range(rows):
        for k in range(3):
            fields[k, i : i + 1, :] = coords_ref[k : k + 1, i * LANES : (i + 1) * LANES]
    group = psi_ref[0]
    cycle_frac, pixel_frac, turns = fields[0], fields[1], fields[2]
    value = v_ref[...]

    def angle(harmonic):
        phase = turns * harmonic.astype(jnp.float32)
        return (2.0 * math.pi) * (phase - jnp.round(phase))

    even = jnp.where(group == 0, 1.0, 2.0 * jnp.sin(angle(group))) * value
    odd = jnp.where(group == nyquist - 1, 1.0, 2.0) * jnp.cos(angle(group + 1)) * value
    pixel = o_ref[...]
    block = (pixel.astype(jnp.float32) * (1.0 / STRIDE) + 0.5 / STRIDE).astype(jnp.int32)
    fields[0] = even * (1.0 - cycle_frac)
    fields[3] = even * cycle_frac
    fields[4] = odd * (1.0 - cycle_frac)
    fields[5] = odd * cycle_frac
    fields[1] = 0.5 * ((pixel - STRIDE * block + 1).astype(jnp.float32) + pixel_frac)
    ids[...] = block
    cube[...] = jnp.zeros_like(cube)
    cycle_ids = lax.broadcasted_iota(jnp.int32, (cycles, LANES), 0)
    columns = 0.5 * lax.broadcasted_iota(jnp.int32, (BLOCK, LANES), 0).astype(jnp.float32)
    width = left.shape[1] // LANES

    def chunk(step, carry):
        for j in range(width):
            row = pl.ds(step * width + j, 1)
            lanes = slice(j * LANES, (j + 1) * LANES)
            cycle = t_ref[row, :]
            here, after = cycle_ids == cycle, cycle_ids == cycle + 1
            hats = [
                jnp.where(here, fields[a, row, :], jnp.where(after, fields[b, row, :], 0.0))
                for a, b in ((0, 3), (4, 5))
            ]
            own = ids[row, :]
            for b in range(blocks):
                mine = own == b
                for c in range(2):
                    start = (2 * b + c) * cycles
                    left[start : start + cycles, lanes] = jnp.where(mine, hats[c], 0.0).astype(
                        jnp.bfloat16
                    )
            offset = columns - fields[1, row, :]
            inner = jnp.maximum(1.0 - offset * offset, 0.0)
            right[:, lanes] = (inner * inner).astype(jnp.bfloat16)
        cube[...] += lax.dot_general(
            left[...], right[...], NT, preferred_element_type=jnp.float32
        )
        return carry

    lax.fori_loop(0, rows // width, chunk, 0)
    copy.wait()
    spread = jnp.concatenate(
        [cube[b * 2 * cycles : (b + 1) * 2 * cycles, :].astype(jnp.bfloat16) for b in range(blocks)],
        axis=1,
    )
    waves = [
        lax.dot_general(table[x], spread, NT, preferred_element_type=jnp.float32) for x in range(2)
    ]
    out_ref[...] = (jnp.concatenate(waves, axis=1) * (1.0 / math.sqrt(nphi))).astype(jnp.bfloat16)


def partial_orders(group, values, coords, cycle_ids, pixels, cycles, nphi, nyquist):
    blocks = -(-nphi // STRIDE)
    rows = values.shape[0] // LANES
    depth = blocks * BLOCK
    table = jnp.asarray(fourier_rows(nphi, blocks))
    chunk = 8 * LANES
    vmem = pl.BlockSpec(memory_space=pltpu.VMEM)
    return pl.pallas_call(
        lambda *refs: deposit_kernel(blocks, cycles, nphi, nyquist, *refs),
        out_shape=jax.ShapeDtypeStruct((nphi // 2, 4 * cycles), jnp.bfloat16),
        in_specs=[pl.BlockSpec(memory_space=pltpu.SMEM)] + [vmem] * 4 + [pl.BlockSpec(memory_space=pl.ANY)],
        out_specs=vmem,
        scratch_shapes=[
            pltpu.VMEM((6, rows, LANES), jnp.float32),
            pltpu.VMEM((rows, LANES), jnp.int32),
            pltpu.VMEM((2 * cycles * blocks, chunk), jnp.bfloat16),
            pltpu.VMEM((BLOCK, chunk), jnp.bfloat16),
            pltpu.VMEM((2 * cycles * blocks, BLOCK), jnp.float32),
            pltpu.VMEM((2, nphi // 2, depth), jnp.bfloat16),
            pltpu.SemaphoreType.DMA,
        ],
        compiler_params=pltpu.CompilerParams(vmem_limit_bytes=48 * 2**20),
    )(
        group,
        values.reshape(rows, LANES),
        coords,
        cycle_ids.reshape(rows, LANES),
        pixels.reshape(rows, LANES),
        table,
    )


def project_kernel(scale, parts_ref, wigner_ref, beam_ref, out_ref, total):
    senders, orders, lanes = parts_ref.shape
    depth = lanes // 2
    pack = BLOCK // depth
    groups = orders // pack
    waves = wigner_ref.shape[2]
    summed = jnp.sum(parts_ref[...].astype(jnp.float32), axis=0).astype(jnp.bfloat16)
    expand = (
        lax.broadcasted_iota(jnp.int32, (2 * orders, orders), 0) // 2
        == lax.broadcasted_iota(jnp.int32, (2 * orders, orders), 1)
    ).astype(jnp.bfloat16)
    tall = jnp.dot(expand, summed, preferred_element_type=jnp.float32)
    row = lax.broadcasted_iota(jnp.int32, (2 * orders, BLOCK), 0)
    lane = lax.broadcasted_iota(jnp.int32, (2 * orders, BLOCK), 1)
    keep = (row % (2 * pack)) == (lane // (depth // 2))
    lhs = [
        jnp.where(keep, jnp.concatenate([tall[:, x * depth : (x + 1) * depth]] * pack, axis=1), 0.0)
        for x in range(2)
    ]
    beam = beam_ref[...] * scale
    weight = jnp.concatenate([beam] * pack, axis=0)
    for g in range(groups):
        rows = slice(2 * pack * g, 2 * pack * (g + 1))
        both = jnp.concatenate([lhs[0][rows], lhs[1][rows]], axis=0).astype(jnp.bfloat16)
        product = jnp.dot(both, wigner_ref[g], preferred_element_type=jnp.float32)
        for x in range(2):
            part = product[x * 2 * pack : (x + 1) * 2 * pack] * weight
            total[x, rows, :] = part
    step = out_ref.shape[2]
    for x in range(2):
        sky = jnp.sum(total[x].reshape(orders, 2, waves), axis=1)
        for k in range(out_ref.shape[0]):
            out_ref[k, x * orders : (x + 1) * orders, :] = sky[:, k * step : (k + 1) * step].astype(
                jnp.bfloat16
            )


def partial_sky(parts, wigner, beam, groups, scale):
    orders, channels, cycles, waves = wigner.shape
    pack = BLOCK // (channels * cycles)
    vmem = pl.BlockSpec(memory_space=pltpu.VMEM)
    return pl.pallas_call(
        lambda *refs: project_kernel(scale, *refs),
        out_shape=jax.ShapeDtypeStruct((groups, 2 * orders, waves // groups), jnp.bfloat16),
        in_specs=[vmem] * 3,
        out_specs=vmem,
        scratch_shapes=[pltpu.VMEM((2, 2 * orders, waves), jnp.float32)],
        compiler_params=pltpu.CompilerParams(vmem_limit_bytes=48 * 2**20),
    )(parts, wigner.reshape(orders // pack, BLOCK, waves), beam)


def body(sample_values, sample_coords, tile_ids, phi_pixels, wigner_table, beam):
    tiles = lax.axis_size("theta")
    groups = lax.axis_size("psi")
    orders, channels, cycles, waves = wigner_table.shape
    nphi = 2 * tiles * orders
    nyquist = groups * channels // 2
    group = lax.axis_index("psi").astype(jnp.int32).reshape(1)
    freq = partial_orders(
        group, sample_values, sample_coords, tile_ids, phi_pixels, cycles, nphi, nyquist
    )
    freq = lax.all_to_all(
        freq.reshape(tiles, orders, freq.shape[1]), "theta", split_axis=0, concat_axis=0, tiled=True
    )
    sky = partial_sky(freq, wigner_table, beam, groups, 1.0 / math.sqrt(groups * channels))
    sky = lax.all_to_all(sky, "psi", split_axis=0, concat_axis=0, tiled=True)
    sky = jnp.sum(sky.astype(jnp.float32), axis=0)
    return sky.reshape(2, orders, waves // groups)


def solution(mesh):
    in_specs = (
        P("theta"),
        P(None, "theta"),
        P("theta", None),
        P("theta"),
        P("theta", "psi", None, None),
        P("psi", None),
    )
    out_specs = P(None, "theta", "psi")
    return jax.shard_map(body, mesh=mesh, in_specs=in_specs, out_specs=out_specs, check_vma=False)
```

```python
import math

import jax
import jax.numpy as jnp
import numpy as np
from jax import lax
from jax.experimental import pallas as pl
from jax.experimental.pallas import tpu as pltpu
from jax.sharding import PartitionSpec as P

LANES = 128
STRIDE = 253
BLOCK = 256
RADIX = 9
NT = (((1,), (1,)), ((), ()))


def fourier_rows(nphi):
    waves = np.arange(nphi // 2).reshape(-1, RADIX).T
    phase = (2.0 * math.pi / nphi) * (waves[:, :, None] * (np.arange(BLOCK) - 1) % nphi)
    return np.concatenate([np.cos(phase), np.sin(phase)], axis=2)


def phase_sums(runs):
    half = RADIX // 2
    even = [runs[b] + runs[RADIX - b] for b in range(1, half + 1)]
    odd = [runs[b] - runs[RADIX - b] for b in range(1, half + 1)]
    sums = []
    for k in range(half + 1):
        real, imag = runs[0], None
        for b in range(1, half + 1):
            turn = 2.0 * math.pi * (k * b % RADIX) / RADIX
            real = real + (even[b - 1] if k == 0 else math.cos(turn) * even[b - 1])
            if k:
                part = -math.sin(turn) * odd[b - 1]
                imag = part if imag is None else imag + part
        sums.append((real, imag))
    return sums


def split(x):
    high = x.astype(jnp.bfloat16)
    return high, (x - high.astype(jnp.float32)).astype(jnp.bfloat16)


def deposit_kernel(
    blocks, cycles, nphi, nyquist, psi_ref, v_hbm, coords_hbm, t_hbm, o_hbm, table_hbm, out_ref,
    values, coords, cycle_of, pixels, fields, left, right, cube, table, spread, sems,
):
    sources = (v_hbm, coords_hbm, o_hbm, t_hbm, table_hbm)
    targets = (values, coords, pixels, cycle_of, table)
    copies = [
        pltpu.make_async_copy(source, target, sems.at[i])
        for i, (source, target) in enumerate(zip(sources, targets))
    ]
    for copy in copies:
        copy.start()
    cube[...] = jnp.zeros_like(cube)
    group = psi_ref[0]
    for copy in copies[:3]:
        copy.wait()
    rows = values.shape[0]
    for i in range(rows):
        for k in range(3):
            fields[k, i : i + 1, :] = coords[k : k + 1, i * LANES : (i + 1) * LANES]
    cycle_frac, pixel_frac, turns = fields[0], fields[1], fields[2]
    value = values[...]

    def angle(harmonic):
        phase = turns * harmonic.astype(jnp.float32)
        return (2.0 * math.pi) * (phase - jnp.round(phase))

    even = jnp.where(group == 0, 1.0, 2.0 * jnp.sin(angle(group))) * value
    odd = jnp.where(group == nyquist - 1, 1.0, 2.0) * jnp.cos(angle(group + 1)) * value
    pixel = pixels[...]
    block = (pixel.astype(jnp.float32) * (1.0 / STRIDE) + 0.5 / STRIDE).astype(jnp.int32)
    fields[0] = even * (1.0 - cycle_frac)
    fields[3] = even * cycle_frac
    fields[4] = odd * (1.0 - cycle_frac)
    fields[5] = odd * cycle_frac
    fields[1] = 0.5 * ((pixel - STRIDE * block + 1).astype(jnp.float32) + pixel_frac)
    pixels[...] = block
    copies[3].wait()
    cycle_ids = lax.broadcasted_iota(jnp.int32, (cycles, LANES), 0)
    columns = 0.5 * lax.broadcasted_iota(jnp.int32, (BLOCK, LANES), 0).astype(jnp.float32)
    width = left.shape[1] // LANES

    def chunk(step, carry):
        for j in range(width):
            row = pl.ds(step * width + j, 1)
            lanes = slice(j * LANES, (j + 1) * LANES)
            cycle = cycle_of[row, :]
            here, after = cycle_ids == cycle, cycle_ids == cycle + 1
            hats = [
                jnp.where(here, fields[a, row, :], jnp.where(after, fields[b, row, :], 0.0))
                for a, b in ((0, 3), (4, 5))
            ]
            own = pixels[row, :]
            for b in range(blocks):
                mine = own == b
                for c in range(2):
                    start = (2 * b + c) * cycles
                    left[start : start + cycles, lanes] = jnp.where(mine, hats[c], 0.0).astype(
                        jnp.bfloat16
                    )
            offset = columns - fields[1, row, :]
            inner = jnp.maximum(1.0 - offset * offset, 0.0)
            right[:, lanes] = (inner * inner).astype(jnp.bfloat16)
        cube[...] += lax.dot_general(
            left[...], right[...], NT, preferred_element_type=jnp.float32
        )
        return carry

    lax.fori_loop(0, rows // width, chunk, 0)
    lines = 2 * cycles
    tiles = nphi // LANES
    sums = [None] * tiles
    blank = jnp.zeros((lines, LANES), jnp.float32)
    for b in range(blocks):
        first, shift = divmod(b * STRIDE, LANES)
        block_rows = cube[b * lines : (b + 1) * lines, :]
        wide = jnp.concatenate([block_rows, blank], axis=1)
        if shift:
            wide = pltpu.roll(wide, shift, 1)
        for k in range(3):
            part = wide[:, k * LANES : (k + 1) * LANES]
            tile = (first + k) % tiles
            sums[tile] = part if sums[tile] is None else sums[tile] + part
    per_run = BLOCK // LANES
    runs = [jnp.concatenate(sums[b * per_run : (b + 1) * per_run], axis=1) for b in range(RADIX)]
    groups = phase_sums(runs)
    copies[4].wait()
    share = out_ref.shape[1] // RADIX
    for m in range(RADIX):
        real, imag = groups[min(m, RADIX - m)]
        imag = jnp.zeros_like(real) if m == 0 else (imag if m <= RADIX // 2 else -imag)
        operand = jnp.concatenate(
            [jnp.concatenate([real, imag], axis=1), jnp.concatenate([imag, -real], axis=1)], axis=0
        ) * (1.0 / math.sqrt(nphi))
        waves = sum(
            lax.dot_general(table[m], part, NT, preferred_element_type=jnp.float32)
            for part in split(operand)
        )
        for d in range(out_ref.shape[0]):
            spread[d, m * share : (m + 1) * share, :] = waves[d * share : (d + 1) * share]
    out_ref[...] = spread[...].astype(jnp.bfloat16)


def partial_orders(group, values, coords, cycle_ids, pixels, cycles, nphi, nyquist, tiles=32):
    blocks = -(-nphi // STRIDE)
    rows = values.shape[0] // LANES
    table = jnp.asarray(fourier_rows(nphi).astype(jnp.bfloat16))
    chunk = 8 * LANES
    vmem = pl.BlockSpec(memory_space=pltpu.VMEM)
    whole = (tiles, nphi // 2 // tiles, 4 * cycles)
    return pl.pallas_call(
        lambda *refs: deposit_kernel(blocks, cycles, nphi, nyquist, *refs),
        out_shape=jax.ShapeDtypeStruct(whole, jnp.bfloat16),
        in_specs=[pl.BlockSpec(memory_space=pltpu.SMEM)] + [pl.BlockSpec(memory_space=pltpu.HBM)] * 5,
        out_specs=vmem,
        scratch_shapes=[
            pltpu.VMEM((rows, LANES), jnp.float32),
            pltpu.VMEM(coords.shape, jnp.float32),
            pltpu.VMEM((rows, LANES), jnp.int32),
            pltpu.VMEM((rows, LANES), jnp.int32),
            pltpu.VMEM((6, rows, LANES), jnp.float32),
            pltpu.VMEM((2 * cycles * blocks, chunk), jnp.bfloat16),
            pltpu.VMEM((BLOCK, chunk), jnp.bfloat16),
            pltpu.VMEM((2 * cycles * blocks, BLOCK), jnp.float32),
            pltpu.VMEM(table.shape, jnp.bfloat16),
            pltpu.VMEM(whole, jnp.float32),
            pltpu.SemaphoreType.DMA((5,)),
        ],
        compiler_params=pltpu.CompilerParams(vmem_limit_bytes=24 * 2**20),
    )(
        group,
        values.reshape(rows, LANES),
        coords,
        cycle_ids.reshape(rows, LANES),
        pixels.reshape(rows, LANES),
        table,
    )


def project_kernel(scale, parts_ref, wigner_ref, beam_ref, out_ref, sky):
    orders, lanes = parts_ref.shape[1:]
    depth = lanes // 2
    pack = BLOCK // depth
    summed = split(jnp.sum(parts_ref[...].astype(jnp.float32), axis=0))
    row = lax.broadcasted_iota(jnp.int32, (2 * orders, orders), 0)
    place = lax.broadcasted_iota(jnp.int32, (2 * orders, orders), 1)
    order = row // 2
    found = (order % RADIX) * (orders // RADIX) + order // RADIX == place
    chosen = [(found & (row % 2 == x)).astype(jnp.bfloat16) for x in range(2)]
    row = lax.broadcasted_iota(jnp.int32, (2 * orders, BLOCK), 0)
    lane = lax.broadcasted_iota(jnp.int32, (2 * orders, BLOCK), 1)
    mine = row // 2 % pack == lane // depth
    second = lane // (depth // 2) % 2
    tops = []
    for part in summed:
        tall = sum(
            jnp.dot(chosen[x], part[:, x * depth : (x + 1) * depth], preferred_element_type=jnp.float32)
            for x in range(2)
        )
        wide = jnp.concatenate([tall] * pack, axis=1)
        tops += [jnp.where(mine & (second == c), wide, 0.0) for c in range(2)]
    beam = beam_ref[...] * scale
    height = 2 * pack
    for g in range(orders // pack):
        rows = slice(height * g, height * (g + 1))
        lhs = jnp.concatenate([top[rows] for top in tops], axis=0).astype(jnp.bfloat16)
        product = jnp.dot(lhs, wigner_ref[g], preferred_element_type=jnp.float32)
        first, other = (
            product[c * height : (c + 1) * height] + product[(c + 2) * height : (c + 3) * height]
            for c in range(2)
        )
        sky[rows, :] = first * beam[0:1] + other * beam[1:2]
    step = sky.shape[1] // out_ref.shape[0]
    over = step - LANES
    fold = LANES // over
    piece = sky.shape[0] // fold
    for k in range(out_ref.shape[0]):
        start = k * step
        rest = [
            sky[j * piece : (j + 1) * piece, start + LANES : start + step] for j in range(fold)
        ]
        out_ref[k] = jnp.concatenate(
            [sky[:, start : start + LANES], jnp.concatenate(rest, axis=1)], axis=0
        ).astype(jnp.bfloat16)


def partial_sky(parts, wigner, beam, groups, scale):
    orders, channels, cycles, waves = wigner.shape
    pack = BLOCK // (channels * cycles)
    vmem = pl.BlockSpec(memory_space=pltpu.VMEM)
    whole = (groups, 2 * orders * (waves // groups) // LANES, LANES)
    return pl.pallas_call(
        lambda *refs: project_kernel(scale, *refs),
        out_shape=jax.ShapeDtypeStruct(whole, jnp.bfloat16),
        in_specs=[vmem] * 3,
        out_specs=vmem,
        scratch_shapes=[pltpu.VMEM((2 * orders, waves), jnp.float32)],
        compiler_params=pltpu.CompilerParams(vmem_limit_bytes=24 * 2**20),
    )(parts, wigner.reshape(orders // pack, BLOCK, waves), beam)


def finish_kernel(parts_ref, out_ref):
    total = jnp.sum(parts_ref[...].astype(jnp.float32), axis=0)
    orders, two, waves = out_ref.shape
    over = waves - LANES
    fold = LANES // over
    main, rest = total[: 2 * orders], total[2 * orders :]
    tail = jnp.concatenate([rest[:, j * over : (j + 1) * over] for j in range(fold)], axis=0)
    out_ref[...] = jnp.concatenate([main, tail], axis=1).reshape(orders, two, waves)


def finish(parts, orders, waves):
    vmem = pl.BlockSpec(memory_space=pltpu.VMEM)
    return pl.pallas_call(
        finish_kernel,
        out_shape=jax.ShapeDtypeStruct((orders, 2, waves), jnp.float32),
        in_specs=[vmem],
        out_specs=vmem,
    )(parts)


def body(sample_values, sample_coords, tile_ids, phi_pixels, wigner_table, beam):
    tiles = lax.axis_size("theta")
    groups = lax.axis_size("psi")
    orders, channels, cycles, waves = wigner_table.shape
    nphi = 2 * tiles * orders
    nyquist = groups * channels // 2
    group = lax.axis_index("psi").astype(jnp.int32).reshape(1)
    freq = partial_orders(
        group, sample_values, sample_coords, tile_ids, phi_pixels, cycles, nphi, nyquist, tiles
    )
    freq = lax.all_to_all(freq, "theta", split_axis=0, concat_axis=0, tiled=True)
    sky = partial_sky(freq, wigner_table, beam, groups, 1.0 / math.sqrt(groups * channels))
    sky = lax.all_to_all(sky, "psi", split_axis=0, concat_axis=0, tiled=True)
    return jnp.moveaxis(finish(sky, orders, waves // groups), 1, 0)


def solution(mesh):
    in_specs = (
        P("theta"),
        P(None, "theta"),
        P("theta", None),
        P("theta"),
        P("theta", "psi", None, None),
        P("psi", None),
    )
    out_specs = P(None, "theta", "psi")
    return jax.shard_map(body, mesh=mesh, in_specs=in_specs, out_specs=out_specs, check_vma=False)
```

```python
import math

import jax
import jax.numpy as jnp
import numpy as np
from jax import lax
from jax.experimental import pallas as pl
from jax.experimental.pallas import tpu as pltpu
from jax.sharding import PartitionSpec as P

LANES = 128
CELL = 32
OWNED = CELL - 3
BLOCK = 256
CELLS = BLOCK // CELL
STRIDE = OWNED * CELLS
RADIX = 9
CHUNK = 1024
NT = (((1,), (1,)), ((), ()))


def fourier_rows(nphi):
    waves = np.arange(nphi // 2).reshape(-1, RADIX).T
    phase = (2.0 * math.pi / nphi) * (waves[:, :, None] * (np.arange(BLOCK) - 1) % nphi)
    return np.concatenate([np.cos(phase), np.sin(phase)], axis=2)


def phase_sums(runs):
    half = RADIX // 2
    even = [runs[b] + runs[RADIX - b] for b in range(1, half + 1)]
    odd = [runs[b] - runs[RADIX - b] for b in range(1, half + 1)]
    sums = []
    for k in range(half + 1):
        real, imag = runs[0], None
        for b in range(1, half + 1):
            turn = 2.0 * math.pi * (k * b % RADIX) / RADIX
            real = real + (even[b - 1] if k == 0 else math.cos(turn) * even[b - 1])
            if k:
                part = -math.sin(turn) * odd[b - 1]
                imag = part if imag is None else imag + part
        sums.append((real, imag))
    return sums


def split(x):
    high = x.astype(jnp.bfloat16)
    return high, (x - high.astype(jnp.float32)).astype(jnp.bfloat16)


def deposit_kernel(
    blocks, cycles, nphi, nyquist, psi_ref, v_hbm, coords_hbm, t_hbm, o_hbm, table_hbm, wigner_hbm,
    beam_hbm, out_ref, wigner, beam, values, coords, cycle_of, pixels, fields, left, right, cube,
    table, spread, sems,
):
    sources = (v_hbm, coords_hbm, o_hbm, t_hbm, table_hbm, beam_hbm, wigner_hbm)
    targets = (values, coords, pixels, cycle_of, table, beam, wigner)
    copies = [
        pltpu.make_async_copy(source, target, sems.at[i])
        for i, (source, target) in enumerate(zip(sources, targets))
    ]
    for copy in copies:
        copy.start()
    cube[...] = jnp.zeros_like(cube)
    group = psi_ref[0]
    for copy in copies[:3]:
        copy.wait()
    rows = values.shape[0]
    for i in range(rows):
        for k in range(3):
            fields[k, i : i + 1, :] = coords[k : k + 1, i * LANES : (i + 1) * LANES]
    cycle_frac, pixel_frac, turns = fields[0], fields[1], fields[2]
    value = values[...]

    def angle(harmonic):
        phase = turns * harmonic.astype(jnp.float32)
        return (2.0 * math.pi) * (phase - jnp.round(phase))

    even = jnp.where(group == 0, 1.0, 2.0 * jnp.sin(angle(group))) * value
    odd = jnp.where(group == nyquist - 1, 1.0, 2.0) * jnp.cos(angle(group + 1)) * value
    pixel = pixels[...]
    cell = (pixel.astype(jnp.float32) * (1.0 / OWNED) + 0.5 / OWNED).astype(jnp.int32)
    fields[0] = even * (1.0 - cycle_frac)
    fields[3] = even * cycle_frac
    fields[4] = odd * (1.0 - cycle_frac)
    fields[5] = odd * cycle_frac
    fields[1] = 0.5 * ((pixel - OWNED * cell + 1).astype(jnp.float32) + pixel_frac)
    fields[2] = (cell // CELLS).astype(jnp.float32)
    fields[6] = (cell % CELLS).astype(jnp.float32)
    copies[3].wait()
    cycle_ids = lax.broadcasted_iota(jnp.int32, (cycles, LANES), 0)
    columns = 0.5 * lax.broadcasted_iota(jnp.int32, (CELL, LANES), 0).astype(jnp.float32)
    width = left.shape[2] // LANES

    def fill(step, slot):
        for j in range(width):
            row = pl.ds(step * width + j, 1)
            lanes = slice(j * LANES, (j + 1) * LANES)
            cycle = cycle_of[row, :]
            here, after = cycle_ids == cycle, cycle_ids == cycle + 1
            hats = [
                jnp.where(here, fields[a, row, :], jnp.where(after, fields[b, row, :], 0.0))
                for a, b in ((0, 3), (4, 5))
            ]
            own, within = (
                jnp.broadcast_to(fields[k, row, :], (CELL, LANES)).astype(jnp.bfloat16)
                for k in (2, 6)
            )
            hats = [hat.astype(jnp.bfloat16) for hat in hats]
            for b in range(blocks):
                mine = own == jnp.bfloat16(b)
                for c in range(2):
                    start = (2 * b + c) * cycles
                    left[slot, start : start + cycles, lanes] = jnp.where(mine, hats[c], jnp.bfloat16(0))
            offset = columns - fields[1, row, :]
            inner = jnp.maximum(1.0 - offset * offset, 0.0)
            taps = (inner * inner).astype(jnp.bfloat16)
            for q in range(CELLS):
                right[slot, q * CELL : (q + 1) * CELL, lanes] = jnp.where(
                    within == jnp.bfloat16(q), taps, jnp.bfloat16(0)
                )

    def add(slot):
        cube[...] += lax.dot_general(
            left[slot], right[slot], NT, preferred_element_type=jnp.float32
        )

    steps = rows // width
    fill(0, 0)

    def pair(step, carry):
        fill(2 * step + 1, 1)
        add(0)
        fill(jnp.minimum(2 * step + 2, steps - 1), 0)
        add(1)
        return carry

    lax.fori_loop(0, steps // 2, pair, 0)
    source = lax.broadcasted_iota(jnp.int32, (BLOCK, BLOCK), 0)
    target = lax.broadcasted_iota(jnp.int32, (BLOCK, BLOCK), 1)
    join = (source - 3 * (source // CELL) == target).astype(jnp.bfloat16)
    cube[...] = sum(
        jnp.dot(part, join, preferred_element_type=jnp.float32) for part in split(cube[...])
    )
    lines = 2 * cycles
    tiles = nphi // LANES
    sums = [None] * tiles
    blank = jnp.zeros((lines, LANES), jnp.float32)
    for b in range(blocks):
        first, shift = divmod(b * STRIDE, LANES)
        block_rows = cube[b * lines : (b + 1) * lines, :]
        wide = jnp.concatenate([block_rows, blank], axis=1)
        if shift:
            wide = pltpu.roll(wide, shift, 1)
        for k in range(3):
            part = wide[:, k * LANES : (k + 1) * LANES]
            tile = (first + k) % tiles
            sums[tile] = part if sums[tile] is None else sums[tile] + part
    per_run = BLOCK // LANES
    runs = [jnp.concatenate(sums[b * per_run : (b + 1) * per_run], axis=1) for b in range(RADIX)]
    groups = phase_sums(runs)
    copies[4].wait()
    share = out_ref.shape[1] // RADIX
    for m in range(RADIX):
        real, imag = groups[min(m, RADIX - m)]
        imag = jnp.zeros_like(real) if m == 0 else (imag if m <= RADIX // 2 else -imag)
        operand = jnp.concatenate(
            [jnp.concatenate([real, imag], axis=1), jnp.concatenate([imag, -real], axis=1)], axis=0
        ) * (1.0 / math.sqrt(nphi))
        waves_m = table[m].astype(jnp.bfloat16)
        waves = sum(
            lax.dot_general(waves_m, part, NT, preferred_element_type=jnp.float32)
            for part in split(operand)
        )
        for d in range(out_ref.shape[0]):
            spread[d, m * share : (m + 1) * share, :] = waves[d * share : (d + 1) * share]
    out_ref[...] = spread[...].astype(jnp.bfloat16)
    for copy in copies[5:]:
        copy.wait()


def partial_orders(group, values, coords, cycle_ids, pixels, wigner, beam, nphi, nyquist, tiles):
    orders, channels, cycles, waves = wigner.shape
    blocks = -(-nphi // STRIDE)
    rows = values.shape[0] // LANES
    table = jnp.asarray(fourier_rows(nphi).astype(np.float32))
    vmem = pl.BlockSpec(memory_space=pltpu.VMEM)
    whole = (tiles, orders, 2 * channels * cycles)
    wigner = wigner.reshape(orders * channels * cycles // BLOCK, BLOCK, waves)
    operands = (
        values.reshape(rows, LANES),
        coords,
        cycle_ids.reshape(rows, LANES),
        pixels.reshape(rows, LANES),
        table,
        wigner,
        beam,
    )
    return pl.pallas_call(
        lambda *refs: deposit_kernel(blocks, cycles, nphi, nyquist, *refs),
        out_shape=[
            pltpu.VMEM(whole, jnp.bfloat16),
            pltpu.VMEM(wigner.shape, wigner.dtype),
            pltpu.VMEM(beam.shape, beam.dtype),
        ],
        in_specs=[pl.BlockSpec(memory_space=pltpu.SMEM)]
        + [pl.BlockSpec(memory_space=pltpu.HBM)] * len(operands),
        out_specs=[vmem] * 3,
        scratch_shapes=[
            pltpu.VMEM((rows, LANES), jnp.float32),
            pltpu.VMEM(coords.shape, jnp.float32),
            pltpu.VMEM((rows, LANES), jnp.int32),
            pltpu.VMEM((rows, LANES), jnp.int32),
            pltpu.VMEM((7, rows, LANES), jnp.float32),
            pltpu.VMEM((2, channels * cycles * blocks, CHUNK), jnp.bfloat16),
            pltpu.VMEM((2, BLOCK, CHUNK), jnp.bfloat16),
            pltpu.VMEM((channels * cycles * blocks, BLOCK), jnp.float32),
            pltpu.VMEM(table.shape, jnp.float32),
            pltpu.VMEM(whole, jnp.float32),
            pltpu.SemaphoreType.DMA((len(operands),)),
        ],
        compiler_params=pltpu.CompilerParams(vmem_limit_bytes=40 * 2**20),
    )(group, *[pltpu.with_memory_space_constraint(x, pltpu.HBM) for x in operands])


def project_kernel(scale, parts_ref, wigner_ref, beam_ref, out_ref, sky):
    orders, lanes = parts_ref.shape[1:]
    depth = lanes // 2
    pack = BLOCK // depth
    summed = split(jnp.sum(parts_ref[...].astype(jnp.float32), axis=0))
    row = lax.broadcasted_iota(jnp.int32, (2 * orders, orders), 0)
    place = lax.broadcasted_iota(jnp.int32, (2 * orders, orders), 1)
    order = row // 2
    found = (order % RADIX) * (orders // RADIX) + order // RADIX == place
    chosen = [(found & (row % 2 == x)).astype(jnp.bfloat16) for x in range(2)]
    row = lax.broadcasted_iota(jnp.int32, (2 * orders, BLOCK), 0)
    lane = lax.broadcasted_iota(jnp.int32, (2 * orders, BLOCK), 1)
    mine = row // 2 % pack == lane // depth
    second = lane // (depth // 2) % 2
    tops = []
    for part in summed:
        tall = sum(
            jnp.dot(chosen[x], part[:, x * depth : (x + 1) * depth], preferred_element_type=jnp.float32)
            for x in range(2)
        )
        wide = jnp.concatenate([tall] * pack, axis=1)
        tops += [jnp.where(mine & (second == c), wide, 0.0) for c in range(2)]
    beam = beam_ref[...] * scale
    height = 2 * pack
    for g in range(orders // pack):
        rows = slice(height * g, height * (g + 1))
        lhs = jnp.concatenate([top[rows] for top in tops], axis=0).astype(jnp.bfloat16)
        product = jnp.dot(lhs, wigner_ref[g], preferred_element_type=jnp.float32)
        first, other = (
            product[c * height : (c + 1) * height] + product[(c + 2) * height : (c + 3) * height]
            for c in range(2)
        )
        sky[rows, :] = first * beam[0:1] + other * beam[1:2]
    step = sky.shape[1] // out_ref.shape[0]
    over = step - LANES
    fold = LANES // over
    piece = sky.shape[0] // fold
    for k in range(out_ref.shape[0]):
        start = k * step
        rest = [
            sky[j * piece : (j + 1) * piece, start + LANES : start + step] for j in range(fold)
        ]
        out_ref[k] = jnp.concatenate(
            [sky[:, start : start + LANES], jnp.concatenate(rest, axis=1)], axis=0
        ).astype(jnp.bfloat16)


def partial_sky(parts, wigner, beam, groups, scale):
    orders, waves = parts.shape[1], beam.shape[1]
    vmem = pl.BlockSpec(memory_space=pltpu.VMEM)
    whole = (groups, 2 * orders * (waves // groups) // LANES, LANES)
    return pl.pallas_call(
        lambda *refs: project_kernel(scale, *refs),
        out_shape=jax.ShapeDtypeStruct(whole, jnp.bfloat16),
        in_specs=[vmem] * 3,
        out_specs=vmem,
        scratch_shapes=[pltpu.VMEM((2 * orders, waves), jnp.float32)],
        compiler_params=pltpu.CompilerParams(vmem_limit_bytes=16 * 2**20),
    )(parts, wigner, beam)


def finish_kernel(parts_ref, out_ref):
    total = jnp.sum(parts_ref[...].astype(jnp.float32), axis=0)
    orders, two, waves = out_ref.shape
    over = waves - LANES
    fold = LANES // over
    main, rest = total[: 2 * orders], total[2 * orders :]
    tail = jnp.concatenate([rest[:, j * over : (j + 1) * over] for j in range(fold)], axis=0)
    out_ref[...] = jnp.concatenate([main, tail], axis=1).reshape(orders, two, waves)


def finish(parts, orders, waves):
    vmem = pl.BlockSpec(memory_space=pltpu.VMEM)
    return pl.pallas_call(
        finish_kernel,
        out_shape=jax.ShapeDtypeStruct((orders, 2, waves), jnp.float32),
        in_specs=[vmem],
        out_specs=vmem,
    )(parts)


def body(sample_values, sample_coords, tile_ids, phi_pixels, wigner_table, beam):
    tiles = lax.axis_size("theta")
    groups = lax.axis_size("psi")
    orders, channels, cycles, waves = wigner_table.shape
    nphi = 2 * tiles * orders
    nyquist = groups * channels // 2
    group = lax.axis_index("psi").astype(jnp.int32).reshape(1)
    samples = (sample_values, sample_coords, tile_ids, phi_pixels)
    freq, wigner, beam = partial_orders(
        group, *samples, wigner_table, beam, nphi, nyquist, tiles
    )
    freq = lax.all_to_all(freq, "theta", split_axis=0, concat_axis=0, tiled=True)
    sky = partial_sky(freq, wigner, beam, groups, 1.0 / math.sqrt(groups * channels))
    sky = lax.all_to_all(sky, "psi", split_axis=0, concat_axis=0, tiled=True)
    return jnp.moveaxis(finish(sky, orders, waves // groups), 1, 0)


def solution(mesh):
    in_specs = (
        P("theta"),
        P(None, "theta"),
        P("theta", None),
        P("theta"),
        P("theta", "psi", None, None),
        P("psi", None),
    )
    out_specs = P(None, "theta", "psi")
    return jax.shard_map(body, mesh=mesh, in_specs=in_specs, out_specs=out_specs, check_vma=False)
```

```python
import math

import jax
import jax.numpy as jnp
import numpy as np
from jax import lax
from jax.experimental import pallas as pl
from jax.experimental.pallas import tpu as pltpu
from jax.sharding import PartitionSpec as P

LANES = 128
CELL = 32
OWNED = CELL - 3
BLOCK = 256
CELLS = BLOCK // CELL
STRIDE = OWNED * CELLS
RADIX = 9
CHUNK = 4096
NT = (((1,), (1,)), ((), ()))


def members(k):
    return [k] if k == 0 else [k, RADIX - k]


def fourier_rows(nphi):
    tables = []
    for k in range(RADIX // 2 + 1):
        for m in members(k):
            waves = np.arange(m, nphi // 2, RADIX)
            phase = (2.0 * math.pi / nphi) * (waves[:, None] * (np.arange(BLOCK) - 1) % nphi)
            tables.append(
                np.concatenate([np.cos(phase), (1.0 if m == k else -1.0) * np.sin(phase)], axis=1)
            )
    return np.concatenate(tables, axis=0)


def phase_sums(runs):
    half = RADIX // 2
    even = [runs[b] + runs[RADIX - b] for b in range(1, half + 1)]
    odd = [runs[b] - runs[RADIX - b] for b in range(1, half + 1)]
    sums = []
    for k in range(half + 1):
        real, imag = runs[0], None
        for b in range(1, half + 1):
            turn = 2.0 * math.pi * (k * b % RADIX) / RADIX
            real = real + (even[b - 1] if k == 0 else math.cos(turn) * even[b - 1])
            if k:
                part = -math.sin(turn) * odd[b - 1]
                imag = part if imag is None else imag + part
        sums.append((real, imag))
    return sums


def sine_of_turns(x):
    x = jnp.where(jnp.abs(x) > 0.25, jnp.where(x > 0, 0.5, -0.5) - x, x)
    y = (2.0 * math.pi) * x
    square = y * y
    total = jnp.full_like(y, -1.0 / math.factorial(11))
    for k in (9, 7, 5, 3, 1):
        total = total * square + (-1.0) ** (k // 2) / math.factorial(k)
    return total * y


def split(x):
    high = x.astype(jnp.bfloat16)
    return high, (x - high.astype(jnp.float32)).astype(jnp.bfloat16)


def deposit_kernel(
    blocks, cycles, nphi, nyquist, psi_ref, v_hbm, coords_hbm, t_hbm, o_hbm, table_hbm, wigner_hbm,
    beam_hbm, out_ref, wigner, beam, values, coords, cycle_of, pixels, fields, left, right, cube,
    table, spread, sems,
):
    sources = (v_hbm, coords_hbm, o_hbm, t_hbm, table_hbm, beam_hbm, wigner_hbm)
    targets = (values, coords, pixels, cycle_of, table, beam, wigner)
    copies = [
        pltpu.make_async_copy(source, target, sems.at[i])
        for i, (source, target) in enumerate(zip(sources, targets))
    ]
    for copy in copies:
        copy.start()
    cube[...] = jnp.zeros_like(cube)
    group = psi_ref[0]
    for copy in copies[:3]:
        copy.wait()
    rows = values.shape[0]
    for i in range(rows):
        for k in range(3):
            fields[k, i : i + 1, :] = coords[k : k + 1, i * LANES : (i + 1) * LANES]
    cycle_frac, pixel_frac, turns = fields[0], fields[1], fields[2]
    value = values[...]

    def sine(harmonic, shift):
        phase = turns * harmonic.astype(jnp.float32)
        phase = phase - jnp.round(phase) + shift
        return sine_of_turns(phase - jnp.round(phase))

    even = jnp.where(group == 0, 1.0, 2.0 * sine(group, 0.0)) * value
    odd = jnp.where(group == nyquist - 1, 1.0, 2.0) * sine(group + 1, 0.25) * value
    pixel = pixels[...]
    cell = (pixel.astype(jnp.float32) * (1.0 / OWNED) + 0.5 / OWNED).astype(jnp.int32)
    fields[0] = even * (1.0 - cycle_frac)
    fields[3] = even * cycle_frac
    fields[4] = odd * (1.0 - cycle_frac)
    fields[5] = odd * cycle_frac
    fields[1] = 0.5 * ((pixel - OWNED * cell + 1).astype(jnp.float32) + pixel_frac)
    fields[2] = (cell // CELLS).astype(jnp.float32)
    fields[6] = (cell % CELLS).astype(jnp.float32)
    copies[3].wait()
    cycle_ids = lax.broadcasted_iota(jnp.int32, (cycles, LANES), 0)
    columns = 0.5 * lax.broadcasted_iota(jnp.int32, (CELL, LANES), 0).astype(jnp.float32)
    width = left.shape[1] // LANES

    def chunk(step, carry):
        for j in range(width):
            row = pl.ds(step * width + j, 1)
            lanes = slice(j * LANES, (j + 1) * LANES)
            cycle = cycle_of[row, :]
            here, after = cycle_ids == cycle, cycle_ids == cycle + 1
            hats = [
                jnp.where(here, fields[a, row, :], jnp.where(after, fields[b, row, :], 0.0))
                for a, b in ((0, 3), (4, 5))
            ]
            own, within = (
                jnp.broadcast_to(fields[k, row, :], (CELL, LANES)).astype(jnp.bfloat16)
                for k in (2, 6)
            )
            hats = [hat.astype(jnp.bfloat16) for hat in hats]
            for b in range(blocks):
                mine = own == jnp.bfloat16(b)
                for c in range(2):
                    start = (2 * b + c) * cycles
                    left[start : start + cycles, lanes] = jnp.where(mine, hats[c], jnp.bfloat16(0))
            offset = columns - fields[1, row, :]
            inner = jnp.maximum(1.0 - offset * offset, 0.0)
            taps = (inner * inner).astype(jnp.bfloat16)
            for q in range(CELLS):
                right[q * CELL : (q + 1) * CELL, lanes] = jnp.where(
                    within == jnp.bfloat16(q), taps, jnp.bfloat16(0)
                )
        cube[...] += lax.dot_general(
            left[...], right[...], NT, preferred_element_type=jnp.float32
        )
        return carry

    lax.fori_loop(0, rows // width, chunk, 0)
    source = lax.broadcasted_iota(jnp.int32, (BLOCK, BLOCK), 0)
    target = lax.broadcasted_iota(jnp.int32, (BLOCK, BLOCK), 1)
    join = (source - 3 * (source // CELL) == target).astype(jnp.bfloat16)
    cube[...] = jnp.dot(
        jnp.concatenate(split(cube[...]), axis=1),
        jnp.concatenate([join, join], axis=0),
        preferred_element_type=jnp.float32,
    )
    lines = 2 * cycles
    tiles = nphi // LANES
    sums = [None] * tiles
    blank = jnp.zeros((lines, LANES), jnp.float32)
    for b in range(blocks):
        first, shift = divmod(b * STRIDE, LANES)
        block_rows = cube[b * lines : (b + 1) * lines, :]
        wide = jnp.concatenate([block_rows, blank], axis=1)
        if shift:
            wide = pltpu.roll(wide, shift, 1)
        for k in range(3):
            part = wide[:, k * LANES : (k + 1) * LANES]
            tile = (first + k) % tiles
            sums[tile] = part if sums[tile] is None else sums[tile] + part
    per_run = BLOCK // LANES
    runs = [jnp.concatenate(sums[b * per_run : (b + 1) * per_run], axis=1) for b in range(RADIX)]
    groups = phase_sums(runs)
    copies[4].wait()
    share = out_ref.shape[1] // RADIX
    count = table.shape[0] // RADIX
    conjugate = jnp.where(
        lax.broadcasted_iota(jnp.int32, (1, LANES), 1) < lines, 1.0, -1.0
    )
    start = 0
    for k, (real, imag) in enumerate(groups):
        real = split(real * (1.0 / math.sqrt(nphi)))
        imag = split(jnp.zeros_like(real[0], jnp.float32) if k == 0 else imag * (1.0 / math.sqrt(nphi)))
        operand = jnp.concatenate(
            [
                jnp.concatenate(pair, axis=1)
                for r, i in zip(real, imag)
                for pair in ((r, i), (i, -r))
            ],
            axis=0,
        )
        stop = start + count * len(members(k))
        both = lax.dot_general(
            table[start:stop].astype(jnp.bfloat16), operand, NT, preferred_element_type=jnp.float32
        )
        start = stop
        both = both[:, :LANES] + both[:, LANES:]
        for place, m in enumerate(members(k)):
            waves = both[place * count : (place + 1) * count]
            if place:
                waves = waves * conjugate
            for d in range(out_ref.shape[0]):
                spread[d, m * share : (m + 1) * share, :] = waves[d * share : (d + 1) * share]
    out_ref[...] = spread[...].astype(jnp.bfloat16)
    for copy in copies[5:]:
        copy.wait()


def partial_orders(group, values, coords, cycle_ids, pixels, wigner, beam, nphi, nyquist, tiles):
    orders, channels, cycles, waves = wigner.shape
    blocks = -(-nphi // STRIDE)
    rows = values.shape[0] // LANES
    table = jnp.asarray(fourier_rows(nphi).astype(np.float32))
    vmem = pl.BlockSpec(memory_space=pltpu.VMEM)
    whole = (tiles, orders, 2 * channels * cycles)
    wigner = wigner.reshape(orders * channels * cycles // BLOCK, BLOCK, waves)
    operands = (
        values.reshape(rows, LANES),
        coords,
        cycle_ids.reshape(rows, LANES),
        pixels.reshape(rows, LANES),
        table,
        wigner,
        beam,
    )
    return pl.pallas_call(
        lambda *refs: deposit_kernel(blocks, cycles, nphi, nyquist, *refs),
        out_shape=[
            pltpu.VMEM(whole, jnp.bfloat16),
            pltpu.VMEM(wigner.shape, wigner.dtype),
            pltpu.VMEM(beam.shape, beam.dtype),
        ],
        in_specs=[pl.BlockSpec(memory_space=pltpu.SMEM)]
        + [pl.BlockSpec(memory_space=pltpu.HBM)] * len(operands),
        out_specs=[vmem] * 3,
        scratch_shapes=[
            pltpu.VMEM((rows, LANES), jnp.float32),
            pltpu.VMEM(coords.shape, jnp.float32),
            pltpu.VMEM((rows, LANES), jnp.int32),
            pltpu.VMEM((rows, LANES), jnp.int32),
            pltpu.VMEM((7, rows, LANES), jnp.float32),
            pltpu.VMEM((channels * cycles * blocks, CHUNK), jnp.bfloat16),
            pltpu.VMEM((BLOCK, CHUNK), jnp.bfloat16),
            pltpu.VMEM((channels * cycles * blocks, BLOCK), jnp.float32),
            pltpu.VMEM(table.shape, jnp.float32),
            pltpu.VMEM(whole, jnp.float32),
            pltpu.SemaphoreType.DMA((len(operands),)),
        ],
        compiler_params=pltpu.CompilerParams(vmem_limit_bytes=40 * 2**20),
    )(group, *[pltpu.with_memory_space_constraint(x, pltpu.HBM) for x in operands])


def project_kernel(scale, parts_ref, wigner_ref, beam_ref, out_ref, sky):
    orders, lanes = parts_ref.shape[1:]
    depth = lanes // 2
    pack = BLOCK // depth
    summed = split(jnp.sum(parts_ref[...].astype(jnp.float32), axis=0))
    row = lax.broadcasted_iota(jnp.int32, (2 * orders, orders), 0)
    place = lax.broadcasted_iota(jnp.int32, (2 * orders, orders), 1)
    order = row // 2
    found = (order % RADIX) * (orders // RADIX) + order // RADIX == place
    chosen = [(found & (row % 2 == x)).astype(jnp.bfloat16) for x in range(2)]
    row = lax.broadcasted_iota(jnp.int32, (2 * orders, BLOCK), 0)
    lane = lax.broadcasted_iota(jnp.int32, (2 * orders, BLOCK), 1)
    mine = row // 2 % pack == lane // depth
    second = lane // (depth // 2) % 2
    tops = []
    for part in summed:
        tall = sum(
            jnp.dot(chosen[x], part[:, x * depth : (x + 1) * depth], preferred_element_type=jnp.float32)
            for x in range(2)
        )
        wide = jnp.concatenate([tall] * pack, axis=1)
        tops += [jnp.where(mine & (second == c), wide, 0.0) for c in range(2)]
    beam = beam_ref[...] * scale
    height = 2 * pack
    for g in range(orders // pack):
        rows = slice(height * g, height * (g + 1))
        lhs = jnp.concatenate([top[rows] for top in tops], axis=0).astype(jnp.bfloat16)
        product = jnp.dot(lhs, wigner_ref[g], preferred_element_type=jnp.float32)
        first, other = (
            product[c * height : (c + 1) * height] + product[(c + 2) * height : (c + 3) * height]
            for c in range(2)
        )
        sky[rows, :] = first * beam[0:1] + other * beam[1:2]
    step = sky.shape[1] // out_ref.shape[0]
    over = step - LANES
    fold = LANES // over
    piece = sky.shape[0] // fold
    for k in range(out_ref.shape[0]):
        start = k * step
        rest = [
            sky[j * piece : (j + 1) * piece, start + LANES : start + step] for j in range(fold)
        ]
        out_ref[k] = jnp.concatenate(
            [sky[:, start : start + LANES], jnp.concatenate(rest, axis=1)], axis=0
        ).astype(jnp.bfloat16)


def partial_sky(parts, wigner, beam, groups, scale):
    orders, waves = parts.shape[1], beam.shape[1]
    vmem = pl.BlockSpec(memory_space=pltpu.VMEM)
    whole = (groups, 2 * orders * (waves // groups) // LANES, LANES)
    return pl.pallas_call(
        lambda *refs: project_kernel(scale, *refs),
        out_shape=jax.ShapeDtypeStruct(whole, jnp.bfloat16),
        in_specs=[vmem] * 3,
        out_specs=vmem,
        scratch_shapes=[pltpu.VMEM((2 * orders, waves), jnp.float32)],
        compiler_params=pltpu.CompilerParams(vmem_limit_bytes=16 * 2**20),
    )(parts, wigner, beam)


def finish_kernel(parts_ref, out_ref):
    total = jnp.sum(parts_ref[...].astype(jnp.float32), axis=0)
    orders, two, waves = out_ref.shape
    over = waves - LANES
    fold = LANES // over
    main, rest = total[: 2 * orders], total[2 * orders :]
    tail = jnp.concatenate([rest[:, j * over : (j + 1) * over] for j in range(fold)], axis=0)
    out_ref[...] = jnp.concatenate([main, tail], axis=1).reshape(orders, two, waves)


def finish(parts, orders, waves):
    vmem = pl.BlockSpec(memory_space=pltpu.VMEM)
    return pl.pallas_call(
        finish_kernel,
        out_shape=jax.ShapeDtypeStruct((orders, 2, waves), jnp.float32),
        in_specs=[vmem],
        out_specs=vmem,
        compiler_params=pltpu.CompilerParams(vmem_limit_bytes=2 * 2**20),
    )(parts)


def body(sample_values, sample_coords, tile_ids, phi_pixels, wigner_table, beam):
    tiles = lax.axis_size("theta")
    groups = lax.axis_size("psi")
    orders, channels, cycles, waves = wigner_table.shape
    nphi = 2 * tiles * orders
    nyquist = groups * channels // 2
    group = lax.axis_index("psi").astype(jnp.int32).reshape(1)
    samples = (sample_values, sample_coords, tile_ids, phi_pixels)
    freq, wigner, beam = partial_orders(
        group, *samples, wigner_table, beam, nphi, nyquist, tiles
    )
    freq = lax.all_to_all(freq, "theta", split_axis=0, concat_axis=0, tiled=True)
    sky = partial_sky(freq, wigner, beam, groups, 1.0 / math.sqrt(groups * channels))
    sky = lax.all_to_all(sky, "psi", split_axis=0, concat_axis=0, tiled=True)
    return jnp.moveaxis(finish(sky, orders, waves // groups), 1, 0)


def solution(mesh):
    in_specs = (
        P("theta"),
        P(None, "theta"),
        P("theta", None),
        P("theta"),
        P("theta", "psi", None, None),
        P("psi", None),
    )
    out_specs = P(None, "theta", "psi")
    return jax.shard_map(body, mesh=mesh, in_specs=in_specs, out_specs=out_specs, check_vma=False)
```

```python
import math

import jax
import jax.numpy as jnp
import numpy as np
from jax import lax
from jax.experimental import pallas as pl
from jax.experimental.pallas import tpu as pltpu
from jax.sharding import PartitionSpec as P

LANES = 128
CELL = 32
OWNED = CELL - 3
BLOCK = 256
CELLS = BLOCK // CELL
STRIDE = OWNED * CELLS
RADIX = 9
CHUNK = 4096
NT = (((1,), (1,)), ((), ()))


def members(k):
    return [k] if k == 0 else [k, RADIX - k]


def fourier_rows(nphi):
    tables = []
    for k in range(RADIX // 2 + 1):
        for m in members(k):
            waves = np.arange(m, nphi // 2, RADIX)
            phase = (2.0 * math.pi / nphi) * (waves[:, None] * (np.arange(BLOCK) - 1) % nphi)
            tables.append(
                np.concatenate([np.cos(phase), (1.0 if m == k else -1.0) * np.sin(phase)], axis=1)
            )
    return np.concatenate(tables, axis=0)


def phase_sums(runs):
    half = RADIX // 2
    even = [runs[b] + runs[RADIX - b] for b in range(1, half + 1)]
    odd = [runs[b] - runs[RADIX - b] for b in range(1, half + 1)]
    sums = []
    for k in range(half + 1):
        real, imag = runs[0], None
        for b in range(1, half + 1):
            turn = 2.0 * math.pi * (k * b % RADIX) / RADIX
            real = real + (even[b - 1] if k == 0 else math.cos(turn) * even[b - 1])
            if k:
                part = -math.sin(turn) * odd[b - 1]
                imag = part if imag is None else imag + part
        sums.append((real, imag))
    return sums


def sine_of_turns(x):
    x = jnp.where(jnp.abs(x) > 0.25, jnp.where(x > 0, 0.5, -0.5) - x, x)
    y = (2.0 * math.pi) * x
    square = y * y
    total = jnp.full_like(y, -1.0 / math.factorial(11))
    for k in (9, 7, 5, 3, 1):
        total = total * square + (-1.0) ** (k // 2) / math.factorial(k)
    return total * y


def split(x):
    high = x.astype(jnp.bfloat16)
    return high, (x - high.astype(jnp.float32)).astype(jnp.bfloat16)


def deposit_kernel(
    blocks, cycles, nphi, nyquist, place_ref, v_hbm, coords_hbm, t_hbm, o_hbm, table_hbm, wigner_hbm,
    beam_hbm, own_ref, other_ref, wigner, beam, values, coords, cycle_of, pixels, fields, left, right, cube,
    table, spread, sems,
):
    sources = (v_hbm, coords_hbm, o_hbm, t_hbm, table_hbm, beam_hbm, wigner_hbm)
    targets = (values, coords, pixels, cycle_of, table, beam, wigner)
    copies = [
        pltpu.make_async_copy(source, target, sems.at[i])
        for i, (source, target) in enumerate(zip(sources, targets))
    ]
    for copy in copies:
        copy.start()
    cube[...] = jnp.zeros_like(cube)
    group, core = place_ref[0] >> 1, place_ref[0] & 1
    for copy in copies[:3]:
        copy.wait()
    rows = values.shape[0]
    for i in range(rows):
        for k in range(3):
            fields[k, i : i + 1, :] = coords[k : k + 1, i * LANES : (i + 1) * LANES]
    cycle_frac, pixel_frac, turns = fields[0], fields[1], fields[2]
    value = values[...]

    def sine(harmonic, shift):
        phase = turns * harmonic.astype(jnp.float32)
        phase = phase - jnp.round(phase) + shift
        return sine_of_turns(phase - jnp.round(phase))

    even = jnp.where(group == 0, 1.0, 2.0 * sine(group, 0.0)) * value
    odd = jnp.where(group == nyquist - 1, 1.0, 2.0) * sine(group + 1, 0.25) * value
    pixel = pixels[...]
    cell = (pixel.astype(jnp.float32) * (1.0 / OWNED) + 0.5 / OWNED).astype(jnp.int32)
    fields[0] = even * (1.0 - cycle_frac)
    fields[3] = even * cycle_frac
    fields[4] = odd * (1.0 - cycle_frac)
    fields[5] = odd * cycle_frac
    fields[1] = 0.5 * ((pixel - OWNED * cell + 1).astype(jnp.float32) + pixel_frac)
    fields[2] = (cell // CELLS).astype(jnp.float32)
    fields[6] = (cell % CELLS).astype(jnp.float32)
    copies[3].wait()
    cycle_ids = lax.broadcasted_iota(jnp.int32, (cycles, LANES), 0)
    columns = 0.5 * lax.broadcasted_iota(jnp.int32, (CELL, LANES), 0).astype(jnp.float32)
    width = left.shape[1] // LANES

    def chunk(step, carry):
        for j in range(width):
            row = pl.ds(step * width + j, 1)
            lanes = slice(j * LANES, (j + 1) * LANES)
            cycle = cycle_of[row, :]
            here, after = cycle_ids == cycle, cycle_ids == cycle + 1
            hats = [
                jnp.where(here, fields[a, row, :], jnp.where(after, fields[b, row, :], 0.0))
                for a, b in ((0, 3), (4, 5))
            ]
            own, within = (
                jnp.broadcast_to(fields[k, row, :], (CELL, LANES)).astype(jnp.bfloat16)
                for k in (2, 6)
            )
            hats = [hat.astype(jnp.bfloat16) for hat in hats]
            for b in range(blocks):
                mine = own == jnp.bfloat16(b)
                for c in range(2):
                    start = (2 * b + c) * cycles
                    left[start : start + cycles, lanes] = jnp.where(mine, hats[c], jnp.bfloat16(0))
            offset = columns - fields[1, row, :]
            inner = jnp.maximum(1.0 - offset * offset, 0.0)
            taps = (inner * inner).astype(jnp.bfloat16)
            for q in range(CELLS):
                right[q * CELL : (q + 1) * CELL, lanes] = jnp.where(
                    within == jnp.bfloat16(q), taps, jnp.bfloat16(0)
                )
        cube[...] += lax.dot_general(
            left[...], right[...], NT, preferred_element_type=jnp.float32
        )
        return carry

    lax.fori_loop(0, rows // width, chunk, 0)
    source = lax.broadcasted_iota(jnp.int32, (BLOCK, BLOCK), 0)
    target = lax.broadcasted_iota(jnp.int32, (BLOCK, BLOCK), 1)
    join = (source - 3 * (source // CELL) == target).astype(jnp.bfloat16)
    cube[...] = jnp.dot(
        jnp.concatenate(split(cube[...]), axis=1),
        jnp.concatenate([join, join], axis=0),
        preferred_element_type=jnp.float32,
    )
    lines = 2 * cycles
    tiles = nphi // LANES
    sums = [None] * tiles
    blank = jnp.zeros((lines, LANES), jnp.float32)
    for b in range(blocks):
        first, shift = divmod(b * STRIDE, LANES)
        block_rows = cube[b * lines : (b + 1) * lines, :]
        wide = jnp.concatenate([block_rows, blank], axis=1)
        if shift:
            wide = pltpu.roll(wide, shift, 1)
        for k in range(3):
            part = wide[:, k * LANES : (k + 1) * LANES]
            tile = (first + k) % tiles
            sums[tile] = part if sums[tile] is None else sums[tile] + part
    per_run = BLOCK // LANES
    runs = [jnp.concatenate(sums[b * per_run : (b + 1) * per_run], axis=1) for b in range(RADIX)]
    groups = phase_sums(runs)
    copies[4].wait()
    half, share = own_ref.shape[0], own_ref.shape[1] // RADIX
    count = table.shape[0] // RADIX
    conjugate = jnp.where(
        lax.broadcasted_iota(jnp.int32, (1, LANES), 1) < lines, 1.0, -1.0
    )
    start = 0
    for k, (real, imag) in enumerate(groups):
        real = split(real * (1.0 / math.sqrt(nphi)))
        imag = split(jnp.zeros_like(real[0], jnp.float32) if k == 0 else imag * (1.0 / math.sqrt(nphi)))
        operand = jnp.concatenate(
            [
                jnp.concatenate(pair, axis=1)
                for r, i in zip(real, imag)
                for pair in ((r, i), (i, -r))
            ],
            axis=0,
        )
        stop = start + count * len(members(k))
        both = lax.dot_general(
            table[start:stop].astype(jnp.bfloat16), operand, NT, preferred_element_type=jnp.float32
        )
        start = stop
        both = both[:, :LANES] + both[:, LANES:]
        for place, m in enumerate(members(k)):
            waves = both[place * count : (place + 1) * count]
            if place:
                waves = waves * conjugate
            for d in range(2 * half):
                slot = d % 2 * half + d // 2
                spread[slot, m * share : (m + 1) * share, :] = waves[d * share : (d + 1) * share]
    own_ref[...] = spread[pl.ds(core * half, half)].astype(jnp.bfloat16)
    other_ref[...] = spread[pl.ds((1 - core) * half, half)].astype(jnp.bfloat16)
    for copy in copies[5:]:
        copy.wait()


def partial_orders(place, values, coords, cycle_ids, pixels, wigner, beam, nphi, nyquist, tiles):
    orders, channels, cycles, waves = wigner.shape
    blocks = -(-nphi // STRIDE)
    rows = values.shape[0] // LANES
    table = jnp.asarray(fourier_rows(nphi).astype(np.float32))
    vmem = pl.BlockSpec(memory_space=pltpu.VMEM)
    whole = (tiles, orders, 2 * channels * cycles)
    wigner = wigner.reshape(orders * channels * cycles // BLOCK, BLOCK, waves)
    operands = (
        values.reshape(rows, LANES),
        coords,
        cycle_ids.reshape(rows, LANES),
        pixels.reshape(rows, LANES),
        table,
        wigner,
        beam,
    )
    return pl.pallas_call(
        lambda *refs: deposit_kernel(blocks, cycles, nphi, nyquist, *refs),
        out_shape=[
            pltpu.VMEM((tiles // 2, *whole[1:]), jnp.bfloat16),
            pltpu.VMEM((tiles // 2, *whole[1:]), jnp.bfloat16),
            pltpu.VMEM(wigner.shape, wigner.dtype),
            pltpu.VMEM(beam.shape, beam.dtype),
        ],
        in_specs=[pl.BlockSpec(memory_space=pltpu.SMEM)]
        + [pl.BlockSpec(memory_space=pltpu.HBM)] * len(operands),
        out_specs=[vmem] * 4,
        scratch_shapes=[
            pltpu.VMEM((rows, LANES), jnp.float32),
            pltpu.VMEM(coords.shape, jnp.float32),
            pltpu.VMEM((rows, LANES), jnp.int32),
            pltpu.VMEM((rows, LANES), jnp.int32),
            pltpu.VMEM((7, rows, LANES), jnp.float32),
            pltpu.VMEM((channels * cycles * blocks, CHUNK), jnp.bfloat16),
            pltpu.VMEM((BLOCK, CHUNK), jnp.bfloat16),
            pltpu.VMEM((channels * cycles * blocks, BLOCK), jnp.float32),
            pltpu.VMEM(table.shape, jnp.float32),
            pltpu.VMEM(whole, jnp.float32),
            pltpu.SemaphoreType.DMA((len(operands),)),
        ],
        compiler_params=pltpu.CompilerParams(vmem_limit_bytes=40 * 2**20),
    )(place, *[pltpu.with_memory_space_constraint(x, pltpu.HBM) for x in operands])


def project_kernel(scale, parts_ref, wigner_ref, beam_ref, out_ref, sky):
    orders, lanes = parts_ref.shape[1:]
    depth = lanes // 2
    pack = BLOCK // depth
    summed = split(jnp.sum(parts_ref[...].astype(jnp.float32), axis=0))
    row = lax.broadcasted_iota(jnp.int32, (2 * orders, orders), 0)
    place = lax.broadcasted_iota(jnp.int32, (2 * orders, orders), 1)
    order = row // 2
    found = (order % RADIX) * (orders // RADIX) + order // RADIX == place
    chosen = [(found & (row % 2 == x)).astype(jnp.bfloat16) for x in range(2)]
    row = lax.broadcasted_iota(jnp.int32, (2 * orders, BLOCK), 0)
    lane = lax.broadcasted_iota(jnp.int32, (2 * orders, BLOCK), 1)
    mine = row // 2 % pack == lane // depth
    second = lane // (depth // 2) % 2
    tops = []
    for part in summed:
        tall = sum(
            jnp.dot(chosen[x], part[:, x * depth : (x + 1) * depth], preferred_element_type=jnp.float32)
            for x in range(2)
        )
        wide = jnp.concatenate([tall] * pack, axis=1)
        tops += [jnp.where(mine & (second == c), wide, 0.0) for c in range(2)]
    beam = beam_ref[...] * scale
    height = 2 * pack
    for g in range(orders // pack):
        rows = slice(height * g, height * (g + 1))
        lhs = jnp.concatenate([top[rows] for top in tops], axis=0).astype(jnp.bfloat16)
        product = jnp.dot(lhs, wigner_ref[g], preferred_element_type=jnp.float32)
        first, other = (
            product[c * height : (c + 1) * height] + product[(c + 2) * height : (c + 3) * height]
            for c in range(2)
        )
        sky[rows, :] = first * beam[0:1] + other * beam[1:2]
    step = sky.shape[1] // out_ref.shape[0]
    over = step - LANES
    fold = LANES // over
    piece = sky.shape[0] // fold
    for k in range(out_ref.shape[0]):
        start = k * step
        rest = [
            sky[j * piece : (j + 1) * piece, start + LANES : start + step] for j in range(fold)
        ]
        out_ref[k] = jnp.concatenate(
            [sky[:, start : start + LANES], jnp.concatenate(rest, axis=1)], axis=0
        ).astype(jnp.bfloat16)


def partial_sky(parts, wigner, beam, groups, scale):
    orders, waves = parts.shape[1], beam.shape[1]
    vmem = pl.BlockSpec(memory_space=pltpu.VMEM)
    whole = (groups, 2 * orders * (waves // groups) // LANES, LANES)
    return pl.pallas_call(
        lambda *refs: project_kernel(scale, *refs),
        out_shape=jax.ShapeDtypeStruct(whole, jnp.bfloat16),
        in_specs=[vmem] * 3,
        out_specs=vmem,
        scratch_shapes=[pltpu.VMEM((2 * orders, waves), jnp.float32)],
        compiler_params=pltpu.CompilerParams(vmem_limit_bytes=16 * 2**20),
    )(parts, wigner, beam)


def finish_kernel(parts_ref, out_ref):
    total = jnp.sum(parts_ref[...].astype(jnp.float32), axis=0)
    orders, two, waves = out_ref.shape
    over = waves - LANES
    fold = LANES // over
    main, rest = total[: 2 * orders], total[2 * orders :]
    tail = jnp.concatenate([rest[:, j * over : (j + 1) * over] for j in range(fold)], axis=0)
    out_ref[...] = jnp.concatenate([main, tail], axis=1).reshape(orders, two, waves)


def finish(parts, orders, waves):
    vmem = pl.BlockSpec(memory_space=pltpu.VMEM)
    return pl.pallas_call(
        finish_kernel,
        out_shape=jax.ShapeDtypeStruct((orders, 2, waves), jnp.float32),
        in_specs=[vmem],
        out_specs=vmem,
        compiler_params=pltpu.CompilerParams(vmem_limit_bytes=2 * 2**20),
    )(parts)


def body(sample_values, sample_coords, tile_ids, phi_pixels, wigner_table, beam):
    tiles = lax.axis_size("theta")
    groups = lax.axis_size("psi")
    orders, channels, cycles, waves = wigner_table.shape
    nphi = 2 * tiles * orders
    nyquist = groups * channels // 2
    place = (2 * lax.axis_index("psi") + (lax.axis_index("theta") & 1)).astype(jnp.int32).reshape(1)
    samples = (sample_values, sample_coords, tile_ids, phi_pixels)
    own, other, wigner, beam = partial_orders(
        place, *samples, wigner_table, beam, nphi, nyquist, tiles
    )
    arrived = lax.ppermute(other, "theta", [(i, i ^ 1) for i in range(tiles)])
    freq = (own.astype(jnp.float32) + arrived.astype(jnp.float32)).astype(jnp.bfloat16)
    sides = [list(range(side, tiles, 2)) for side in range(2)]
    freq = lax.all_to_all(
        freq, "theta", split_axis=0, concat_axis=0, axis_index_groups=sides, tiled=True
    )
    sky = partial_sky(freq, wigner, beam, groups, 1.0 / math.sqrt(groups * channels))
    sky = lax.all_to_all(sky, "psi", split_axis=0, concat_axis=0, tiled=True)
    return jnp.moveaxis(finish(sky, orders, waves // groups), 1, 0)


def solution(mesh):
    in_specs = (
        P("theta"),
        P(None, "theta"),
        P("theta", None),
        P("theta"),
        P("theta", "psi", None, None),
        P("psi", None),
    )
    out_specs = P(None, "theta", "psi")
    return jax.shard_map(body, mesh=mesh, in_specs=in_specs, out_specs=out_specs, check_vma=False)
```

```python
import math

import jax
import jax.numpy as jnp
import numpy as np
from jax import lax
from jax.experimental import pallas as pl
from jax.experimental.pallas import tpu as pltpu
from jax.sharding import PartitionSpec as P

LANES = 128
CELL = 32
OWNED = CELL - 3
BLOCK = 256
CELLS = BLOCK // CELL
STRIDE = OWNED * CELLS
RADIX = 9
CHUNK = 4096
NT = (((1,), (1,)), ((), ()))


def members(k):
    return [k] if k == 0 else [k, RADIX - k]


def fourier_rows(nphi):
    tables = []
    for k in range(RADIX // 2 + 1):
        for m in members(k):
            waves = np.arange(m, nphi // 2, RADIX)
            phase = (2.0 * math.pi / nphi) * (waves[:, None] * (np.arange(BLOCK) - 1) % nphi)
            tables.append(
                np.concatenate([np.cos(phase), (1.0 if m == k else -1.0) * np.sin(phase)], axis=1)
            )
    return np.concatenate(tables, axis=0)


def phase_sums(runs):
    half = RADIX // 2
    even = [runs[b] + runs[RADIX - b] for b in range(1, half + 1)]
    odd = [runs[b] - runs[RADIX - b] for b in range(1, half + 1)]
    sums = []
    for k in range(half + 1):
        real, imag = runs[0], None
        for b in range(1, half + 1):
            turn = 2.0 * math.pi * (k * b % RADIX) / RADIX
            real = real + (even[b - 1] if k == 0 else math.cos(turn) * even[b - 1])
            if k:
                part = -math.sin(turn) * odd[b - 1]
                imag = part if imag is None else imag + part
        sums.append((real, imag))
    return sums


def sine_of_turns(x):
    x = jnp.where(jnp.abs(x) > 0.25, jnp.where(x > 0, 0.5, -0.5) - x, x)
    y = (2.0 * math.pi) * x
    square = y * y
    total = jnp.full_like(y, -1.0 / math.factorial(11))
    for k in (9, 7, 5, 3, 1):
        total = total * square + (-1.0) ** (k // 2) / math.factorial(k)
    return total * y


def log2(size):
    assert size == 1 << size.bit_length() - 1
    return size.bit_length() - 1


def split(x):
    high = x.astype(jnp.bfloat16)
    return high, (x - high.astype(jnp.float32)).astype(jnp.bfloat16)


def deposit_kernel(
    blocks, cycles, nphi, nyquist, place_ref, v_hbm, coords_hbm, t_hbm, o_hbm, table_hbm, wigner_hbm,
    beam_hbm, own_ref, other_ref, wigner, beam, values, coords, cycle_of, pixels, fields, left, right, cube,
    table, spread, sems,
):
    sources = (v_hbm, coords_hbm, o_hbm, t_hbm, table_hbm, beam_hbm, wigner_hbm)
    targets = (values, coords, pixels, cycle_of, table, beam, wigner)
    copies = [
        pltpu.make_async_copy(source, target, sems.at[i])
        for i, (source, target) in enumerate(zip(sources, targets))
    ]
    for copy in copies:
        copy.start()
    cube[...] = jnp.zeros_like(cube)
    group, core = place_ref[0] >> 1, place_ref[0] & 1
    for copy in copies[:3]:
        copy.wait()
    rows = values.shape[0]
    for i in range(rows):
        for k in range(3):
            fields[k, i : i + 1, :] = coords[k : k + 1, i * LANES : (i + 1) * LANES]
    cycle_frac, pixel_frac, turns = fields[0], fields[1], fields[2]
    value = values[...]

    def sine(harmonic, shift):
        phase = turns * harmonic.astype(jnp.float32)
        phase = phase - jnp.round(phase) + shift
        return sine_of_turns(phase - jnp.round(phase))

    even = jnp.where(group == 0, 1.0, 2.0 * sine(group, 0.0)) * value
    odd = jnp.where(group == nyquist - 1, 1.0, 2.0) * sine(group + 1, 0.25) * value
    pixel = pixels[...]
    cell = (pixel.astype(jnp.float32) * (1.0 / OWNED) + 0.5 / OWNED).astype(jnp.int32)
    fields[0] = even * (1.0 - cycle_frac)
    fields[3] = even * cycle_frac
    fields[4] = odd * (1.0 - cycle_frac)
    fields[5] = odd * cycle_frac
    fields[1] = 0.5 * ((pixel - OWNED * cell + 1).astype(jnp.float32) + pixel_frac)
    fields[2] = (cell >> log2(CELLS)).astype(jnp.float32)
    fields[6] = (cell & CELLS - 1).astype(jnp.float32)
    copies[3].wait()
    cycle_ids = lax.broadcasted_iota(jnp.int32, (cycles, LANES), 0)
    columns = 0.5 * lax.broadcasted_iota(jnp.int32, (CELL, LANES), 0).astype(jnp.float32)
    width = left.shape[1] // LANES

    def chunk(step, carry):
        for j in range(width):
            row = pl.ds(step * width + j, 1)
            lanes = slice(j * LANES, (j + 1) * LANES)
            cycle = cycle_of[row, :]
            here, after = cycle_ids == cycle, cycle_ids == cycle + 1
            hats = [
                jnp.where(here, fields[a, row, :], jnp.where(after, fields[b, row, :], 0.0))
                for a, b in ((0, 3), (4, 5))
            ]
            own, within = (
                jnp.broadcast_to(fields[k, row, :], (CELL, LANES)).astype(jnp.bfloat16)
                for k in (2, 6)
            )
            hats = [hat.astype(jnp.bfloat16) for hat in hats]
            for b in range(blocks):
                mine = own == jnp.bfloat16(b)
                for c in range(2):
                    start = (2 * b + c) * cycles
                    left[start : start + cycles, lanes] = jnp.where(mine, hats[c], jnp.bfloat16(0))
            offset = columns - fields[1, row, :]
            inner = jnp.maximum(1.0 - offset * offset, 0.0)
            taps = (inner * inner).astype(jnp.bfloat16)
            for q in range(CELLS):
                right[q * CELL : (q + 1) * CELL, lanes] = jnp.where(
                    within == jnp.bfloat16(q), taps, jnp.bfloat16(0)
                )
        cube[...] += lax.dot_general(
            left[...], right[...], NT, preferred_element_type=jnp.float32
        )
        return carry

    lax.fori_loop(0, rows // width, chunk, 0)
    source = lax.broadcasted_iota(jnp.int32, (BLOCK, BLOCK), 0)
    target = lax.broadcasted_iota(jnp.int32, (BLOCK, BLOCK), 1)
    join = (source - 3 * (source >> log2(CELL)) == target).astype(jnp.bfloat16)
    cube[...] = jnp.dot(
        jnp.concatenate(split(cube[...]), axis=1),
        jnp.concatenate([join, join], axis=0),
        preferred_element_type=jnp.float32,
    )
    lines = 2 * cycles
    tiles = nphi // LANES
    sums = [None] * tiles
    blank = jnp.zeros((lines, LANES), jnp.float32)
    for b in range(blocks):
        first, shift = divmod(b * STRIDE, LANES)
        block_rows = cube[b * lines : (b + 1) * lines, :]
        wide = jnp.concatenate([block_rows, blank], axis=1)
        if shift:
            wide = pltpu.roll(wide, shift, 1)
        for k in range(3):
            part = wide[:, k * LANES : (k + 1) * LANES]
            tile = (first + k) % tiles
            sums[tile] = part if sums[tile] is None else sums[tile] + part
    per_run = BLOCK // LANES
    runs = [jnp.concatenate(sums[b * per_run : (b + 1) * per_run], axis=1) for b in range(RADIX)]
    groups = phase_sums(runs)
    copies[4].wait()
    half, share = own_ref.shape[0], own_ref.shape[1] // RADIX
    count = table.shape[0] // RADIX
    conjugate = jnp.where(
        lax.broadcasted_iota(jnp.int32, (1, LANES), 1) < lines, 1.0, -1.0
    )
    start = 0
    for k, (real, imag) in enumerate(groups):
        real = split(real * (1.0 / math.sqrt(nphi)))
        imag = split(jnp.zeros_like(real[0], jnp.float32) if k == 0 else imag * (1.0 / math.sqrt(nphi)))
        operand = jnp.concatenate(
            [
                jnp.concatenate(pair, axis=1)
                for r, i in zip(real, imag)
                for pair in ((r, i), (i, -r))
            ],
            axis=0,
        )
        stop = start + count * len(members(k))
        both = lax.dot_general(
            table[start:stop].astype(jnp.bfloat16), operand, NT, preferred_element_type=jnp.float32
        )
        start = stop
        both = both[:, :LANES] + both[:, LANES:]
        for place, m in enumerate(members(k)):
            waves = both[place * count : (place + 1) * count]
            if place:
                waves = waves * conjugate
            for d in range(2 * half):
                slot = d % 2 * half + d // 2
                spread[slot, m * share : (m + 1) * share, :] = waves[d * share : (d + 1) * share]
    own_ref[...] = spread[pl.ds(core * half, half)].astype(jnp.bfloat16)
    other_ref[...] = spread[pl.ds((1 - core) * half, half)].astype(jnp.bfloat16)
    for copy in copies[5:]:
        copy.wait()


def partial_orders(place, values, coords, cycle_ids, pixels, wigner, beam, nphi, nyquist, tiles):
    orders, channels, cycles, waves = wigner.shape
    blocks = -(-nphi // STRIDE)
    rows = values.shape[0] // LANES
    table = jnp.asarray(fourier_rows(nphi).astype(np.float32))
    vmem = pl.BlockSpec(memory_space=pltpu.VMEM)
    whole = (tiles, orders, 2 * channels * cycles)
    wigner = wigner.reshape(orders * channels * cycles // BLOCK, BLOCK, waves)
    operands = (
        values.reshape(rows, LANES),
        coords,
        cycle_ids.reshape(rows, LANES),
        pixels.reshape(rows, LANES),
        table,
        wigner,
        beam,
    )
    return pl.pallas_call(
        lambda *refs: deposit_kernel(blocks, cycles, nphi, nyquist, *refs),
        out_shape=[
            pltpu.VMEM((tiles // 2, *whole[1:]), jnp.bfloat16),
            pltpu.VMEM((tiles // 2, *whole[1:]), jnp.bfloat16),
            pltpu.VMEM(wigner.shape, wigner.dtype),
            pltpu.VMEM(beam.shape, beam.dtype),
        ],
        in_specs=[pl.BlockSpec(memory_space=pltpu.SMEM)]
        + [pl.BlockSpec(memory_space=pltpu.HBM)] * len(operands),
        out_specs=[vmem] * 4,
        scratch_shapes=[
            pltpu.VMEM((rows, LANES), jnp.float32),
            pltpu.VMEM(coords.shape, jnp.float32),
            pltpu.VMEM((rows, LANES), jnp.int32),
            pltpu.VMEM((rows, LANES), jnp.int32),
            pltpu.VMEM((7, rows, LANES), jnp.float32),
            pltpu.VMEM((channels * cycles * blocks, CHUNK), jnp.bfloat16),
            pltpu.VMEM((BLOCK, CHUNK), jnp.bfloat16),
            pltpu.VMEM((channels * cycles * blocks, BLOCK), jnp.float32),
            pltpu.VMEM(table.shape, jnp.float32),
            pltpu.VMEM(whole, jnp.float32),
            pltpu.SemaphoreType.DMA((len(operands),)),
        ],
        compiler_params=pltpu.CompilerParams(vmem_limit_bytes=40 * 2**20),
    )(place, *[pltpu.with_memory_space_constraint(x, pltpu.HBM) for x in operands])


def project_kernel(scale, parts_ref, wigner_ref, beam_ref, out_ref, sky, tall):
    orders, lanes = parts_ref.shape[1:]
    depth = lanes // 2
    pack = BLOCK // depth
    summed = jnp.sum(parts_ref[...].astype(jnp.float32), axis=0)
    share = orders // RADIX
    for m in range(RADIX):
        for x in range(2):
            tall[pl.ds(2 * m + x, share, stride=2 * RADIX), :] = summed[
                m * share : (m + 1) * share, x * depth : (x + 1) * depth
            ]
    row = lax.broadcasted_iota(jnp.int32, (2 * orders, BLOCK), 0)
    lane = lax.broadcasted_iota(jnp.int32, (2 * orders, BLOCK), 1)
    mine = (row >> 1 & pack - 1) == lane >> log2(depth)
    second = lane >> log2(depth // 2) & 1
    wide = jnp.where(mine, jnp.concatenate([tall[...]] * pack, axis=1), 0.0)
    tops = [
        jnp.where(second == c, part.astype(jnp.float32), 0.0) for part in split(wide) for c in range(2)
    ]
    beam = beam_ref[...] * scale
    height = 2 * pack
    for g in range(orders // pack):
        rows = slice(height * g, height * (g + 1))
        lhs = jnp.concatenate([top[rows] for top in tops], axis=0).astype(jnp.bfloat16)
        product = jnp.dot(lhs, wigner_ref[g], preferred_element_type=jnp.float32)
        first, other = (
            product[c * height : (c + 1) * height] + product[(c + 2) * height : (c + 3) * height]
            for c in range(2)
        )
        sky[rows, :] = first * beam[0:1] + other * beam[1:2]
    step = sky.shape[1] // out_ref.shape[0]
    over = step - LANES
    fold = LANES // over
    piece = sky.shape[0] // fold
    for k in range(out_ref.shape[0]):
        start = k * step
        rest = [
            sky[j * piece : (j + 1) * piece, start + LANES : start + step] for j in range(fold)
        ]
        out_ref[k] = jnp.concatenate(
            [sky[:, start : start + LANES], jnp.concatenate(rest, axis=1)], axis=0
        ).astype(jnp.bfloat16)


def partial_sky(parts, wigner, beam, groups, scale):
    orders, waves = parts.shape[1], beam.shape[1]
    vmem = pl.BlockSpec(memory_space=pltpu.VMEM)
    whole = (groups, 2 * orders * (waves // groups) // LANES, LANES)
    return pl.pallas_call(
        lambda *refs: project_kernel(scale, *refs),
        out_shape=jax.ShapeDtypeStruct(whole, jnp.bfloat16),
        in_specs=[vmem] * 3,
        out_specs=vmem,
        scratch_shapes=[
            pltpu.VMEM((2 * orders, waves), jnp.float32),
            pltpu.VMEM((2 * orders, parts.shape[2] // 2), jnp.float32),
        ],
        compiler_params=pltpu.CompilerParams(vmem_limit_bytes=16 * 2**20),
    )(parts, wigner, beam)


def finish_kernel(parts_ref, out_ref):
    total = jnp.sum(parts_ref[...].astype(jnp.float32), axis=0)
    orders, two, waves = out_ref.shape
    over = waves - LANES
    fold = LANES // over
    main, rest = total[: 2 * orders], total[2 * orders :]
    tail = jnp.concatenate([rest[:, j * over : (j + 1) * over] for j in range(fold)], axis=0)
    out_ref[...] = jnp.concatenate([main, tail], axis=1).reshape(orders, two, waves)


def finish(parts, orders, waves):
    vmem = pl.BlockSpec(memory_space=pltpu.VMEM)
    return pl.pallas_call(
        finish_kernel,
        out_shape=jax.ShapeDtypeStruct((orders, 2, waves), jnp.float32),
        in_specs=[vmem],
        out_specs=vmem,
        compiler_params=pltpu.CompilerParams(vmem_limit_bytes=2 * 2**20),
    )(parts)


def body(sample_values, sample_coords, tile_ids, phi_pixels, wigner_table, beam):
    tiles = lax.axis_size("theta")
    groups = lax.axis_size("psi")
    orders, channels, cycles, waves = wigner_table.shape
    nphi = 2 * tiles * orders
    nyquist = groups * channels // 2
    place = (2 * lax.axis_index("psi") + (lax.axis_index("theta") & 1)).astype(jnp.int32).reshape(1)
    samples = (sample_values, sample_coords, tile_ids, phi_pixels)
    own, other, wigner, beam = partial_orders(
        place, *samples, wigner_table, beam, nphi, nyquist, tiles
    )
    arrived = lax.ppermute(other, "theta", [(i, i ^ 1) for i in range(tiles)])
    freq = (own.astype(jnp.float32) + arrived.astype(jnp.float32)).astype(jnp.bfloat16)
    sides = [list(range(side, tiles, 2)) for side in range(2)]
    freq = lax.all_to_all(
        freq, "theta", split_axis=0, concat_axis=0, axis_index_groups=sides, tiled=True
    )
    sky = partial_sky(freq, wigner, beam, groups, 1.0 / math.sqrt(groups * channels))
    sky = lax.all_to_all(sky, "psi", split_axis=0, concat_axis=0, tiled=True)
    return jnp.moveaxis(finish(sky, orders, waves // groups), 1, 0)


def solution(mesh):
    in_specs = (
        P("theta"),
        P(None, "theta"),
        P("theta", None),
        P("theta"),
        P("theta", "psi", None, None),
        P("psi", None),
    )
    out_specs = P(None, "theta", "psi")
    return jax.shard_map(body, mesh=mesh, in_specs=in_specs, out_specs=out_specs, check_vma=False)
```

```python
import math

import jax
import jax.numpy as jnp
import numpy as np
from jax import lax
from jax.experimental import pallas as pl
from jax.experimental.pallas import tpu as pltpu
from jax.sharding import PartitionSpec as P

LANES = 128
CELL = 32
OWNED = CELL - 3
BLOCK = 256
CELLS = BLOCK // CELL
STRIDE = OWNED * CELLS
RADIX = 9
CHUNK = 4096
NT = (((1,), (1,)), ((), ()))


def members(k):
    return [k] if k == 0 else [k, RADIX - k]


def fourier_rows(nphi, tiles):
    tables = []
    for k in range(RADIX // 2 + 1):
        for m in members(k):
            waves = np.arange(m, nphi // 2, RADIX)
            phase = (2.0 * math.pi / nphi) * (waves[:, None] * (np.arange(BLOCK) - 1) % nphi)
            tables.append(
                np.concatenate([np.cos(phase), (1.0 if m == k else -1.0) * np.sin(phase)], axis=1)
            )
    sides = [x.reshape(tiles // 2, 2, -1, 2 * BLOCK).swapaxes(0, 1).reshape(2, -1, 2 * BLOCK) for x in tables]
    return np.concatenate(sides, axis=1)


def phase_sums(runs):
    half = RADIX // 2
    even = [runs[b] + runs[RADIX - b] for b in range(1, half + 1)]
    odd = [runs[b] - runs[RADIX - b] for b in range(1, half + 1)]
    sums = []
    for k in range(half + 1):
        real, imag = runs[0], None
        for b in range(1, half + 1):
            turn = 2.0 * math.pi * (k * b % RADIX) / RADIX
            real = real + (even[b - 1] if k == 0 else math.cos(turn) * even[b - 1])
            if k:
                part = -math.sin(turn) * odd[b - 1]
                imag = part if imag is None else imag + part
        sums.append((real, imag))
    return sums


def sine_of_turns(x):
    x = jnp.where(jnp.abs(x) > 0.25, jnp.where(x > 0, 0.5, -0.5) - x, x)
    y = (2.0 * math.pi) * x
    square = y * y
    total = jnp.full_like(y, -1.0 / math.factorial(11))
    for k in (9, 7, 5, 3, 1):
        total = total * square + (-1.0) ** (k // 2) / math.factorial(k)
    return total * y


def log2(size):
    assert size == 1 << size.bit_length() - 1
    return size.bit_length() - 1


def split(x):
    high = x.astype(jnp.bfloat16)
    return high, (x - high.astype(jnp.float32)).astype(jnp.bfloat16)


def transform(table, operands, out_ref, spread):
    owners, share = out_ref.shape[0], out_ref.shape[1] // RADIX
    count = owners * share
    conjugate = jnp.where(
        lax.broadcasted_iota(jnp.int32, (1, LANES), 1) < LANES // 2, 1.0, -1.0
    )
    start = 0
    for k in range(operands.shape[0]):
        stop = start + count * len(members(k))
        both = lax.dot_general(
            table[start:stop].astype(jnp.bfloat16),
            operands[k],
            NT,
            preferred_element_type=jnp.float32,
        )
        start = stop
        both = both[:, :LANES] + both[:, LANES:]
        for place, m in enumerate(members(k)):
            waves = both[place * count : (place + 1) * count]
            if place:
                waves = waves * conjugate
            for d in range(owners):
                spread[d, m * share : (m + 1) * share, :] = waves[d * share : (d + 1) * share]
    out_ref[...] = spread[...].astype(jnp.bfloat16)


def own_kernel(place_ref, table, operands, own_ref, spread):
    transform(table.at[place_ref[0] & 1], operands, own_ref, spread)


def own_orders(place, table, operands, shape):
    vmem = pl.BlockSpec(memory_space=pltpu.VMEM)
    return pl.pallas_call(
        own_kernel,
        out_shape=pltpu.VMEM(shape, jnp.bfloat16),
        in_specs=[pl.BlockSpec(memory_space=pltpu.SMEM), vmem, vmem],
        out_specs=vmem,
        scratch_shapes=[pltpu.VMEM(shape, jnp.float32)],
        compiler_params=pltpu.CompilerParams(vmem_limit_bytes=8 * 2**20),
    )(place, table, operands)


def deposit_kernel(
    blocks, cycles, nphi, nyquist, place_ref, v_hbm, coords_hbm, t_hbm, o_hbm, table_hbm, wigner_hbm,
    beam_hbm, other_ref, operands, table, wigner, beam, values, coords, cycle_of, pixels, fields,
    left, right, cube, spread, sems,
):
    sources = (v_hbm, coords_hbm, o_hbm, t_hbm, table_hbm, beam_hbm, wigner_hbm)
    targets = (values, coords, pixels, cycle_of, table, beam, wigner)
    copies = [
        pltpu.make_async_copy(source, target, sems.at[i])
        for i, (source, target) in enumerate(zip(sources, targets))
    ]
    for copy in copies:
        copy.start()
    cube[...] = jnp.zeros_like(cube)
    group, core = place_ref[0] >> 1, place_ref[0] & 1
    for copy in copies[:3]:
        copy.wait()
    rows = values.shape[0]
    for i in range(rows):
        for k in range(3):
            fields[k, i : i + 1, :] = coords[k : k + 1, i * LANES : (i + 1) * LANES]
    cycle_frac, pixel_frac, turns = fields[0], fields[1], fields[2]
    value = values[...]

    def sine(harmonic, shift):
        phase = turns * harmonic.astype(jnp.float32)
        phase = phase - jnp.round(phase) + shift
        return sine_of_turns(phase - jnp.round(phase))

    even = jnp.where(group == 0, 1.0, 2.0 * sine(group, 0.0)) * value
    odd = jnp.where(group == nyquist - 1, 1.0, 2.0) * sine(group + 1, 0.25) * value
    pixel = pixels[...]
    cell = (pixel.astype(jnp.float32) * (1.0 / OWNED) + 0.5 / OWNED).astype(jnp.int32)
    fields[0] = even * (1.0 - cycle_frac)
    fields[3] = even * cycle_frac
    fields[4] = odd * (1.0 - cycle_frac)
    fields[5] = odd * cycle_frac
    fields[1] = 0.5 * ((pixel - OWNED * cell + 1).astype(jnp.float32) + pixel_frac)
    fields[2] = (cell >> log2(CELLS)).astype(jnp.float32)
    fields[6] = (cell & CELLS - 1).astype(jnp.float32)
    copies[3].wait()
    cycle_ids = lax.broadcasted_iota(jnp.int32, (cycles, LANES), 0)
    columns = 0.5 * lax.broadcasted_iota(jnp.int32, (CELL, LANES), 0).astype(jnp.float32)
    width = left.shape[1] // LANES

    def chunk(step, carry):
        for j in range(width):
            row = pl.ds(step * width + j, 1)
            lanes = slice(j * LANES, (j + 1) * LANES)
            cycle = cycle_of[row, :]
            here, after = cycle_ids == cycle, cycle_ids == cycle + 1
            hats = [
                jnp.where(here, fields[a, row, :], jnp.where(after, fields[b, row, :], 0.0))
                for a, b in ((0, 3), (4, 5))
            ]
            own, within = (
                jnp.broadcast_to(fields[k, row, :], (CELL, LANES)).astype(jnp.bfloat16)
                for k in (2, 6)
            )
            hats = [hat.astype(jnp.bfloat16) for hat in hats]
            for b in range(blocks):
                mine = own == jnp.bfloat16(b)
                for c in range(2):
                    start = (2 * b + c) * cycles
                    left[start : start + cycles, lanes] = jnp.where(mine, hats[c], jnp.bfloat16(0))
            offset = columns - fields[1, row, :]
            inner = jnp.maximum(1.0 - offset * offset, 0.0)
            taps = (inner * inner).astype(jnp.bfloat16)
            for q in range(CELLS):
                right[q * CELL : (q + 1) * CELL, lanes] = jnp.where(
                    within == jnp.bfloat16(q), taps, jnp.bfloat16(0)
                )
        cube[...] += lax.dot_general(
            left[...], right[...], NT, preferred_element_type=jnp.float32
        )
        return carry

    lax.fori_loop(0, rows // width, chunk, 0)
    source = lax.broadcasted_iota(jnp.int32, (BLOCK, BLOCK), 0)
    target = lax.broadcasted_iota(jnp.int32, (BLOCK, BLOCK), 1)
    join = (source - 3 * (source >> log2(CELL)) == target).astype(jnp.bfloat16)
    cube[...] = jnp.dot(
        jnp.concatenate(split(cube[...]), axis=1),
        jnp.concatenate([join, join], axis=0),
        preferred_element_type=jnp.float32,
    )
    lines = 2 * cycles
    tiles = nphi // LANES
    sums = [None] * tiles
    blank = jnp.zeros((lines, LANES), jnp.float32)
    for b in range(blocks):
        first, shift = divmod(b * STRIDE, LANES)
        block_rows = cube[b * lines : (b + 1) * lines, :]
        wide = jnp.concatenate([block_rows, blank], axis=1)
        if shift:
            wide = pltpu.roll(wide, shift, 1)
        for k in range(3):
            part = wide[:, k * LANES : (k + 1) * LANES]
            tile = (first + k) % tiles
            sums[tile] = part if sums[tile] is None else sums[tile] + part
    per_run = BLOCK // LANES
    runs = [jnp.concatenate(sums[b * per_run : (b + 1) * per_run], axis=1) for b in range(RADIX)]
    groups = phase_sums(runs)
    copies[4].wait()
    for k, (real, imag) in enumerate(groups):
        real = split(real * (1.0 / math.sqrt(nphi)))
        imag = split(jnp.zeros_like(real[0], jnp.float32) if k == 0 else imag * (1.0 / math.sqrt(nphi)))
        operands[k] = jnp.concatenate(
            [
                jnp.concatenate(pair, axis=1)
                for r, i in zip(real, imag)
                for pair in ((r, i), (i, -r))
            ],
            axis=0,
        )
    transform(table.at[1 - core], operands, other_ref, spread)
    for copy in copies[5:]:
        copy.wait()


def partial_orders(place, values, coords, cycle_ids, pixels, wigner, beam, nphi, nyquist, tiles):
    orders, channels, cycles, waves = wigner.shape
    blocks = -(-nphi // STRIDE)
    rows = values.shape[0] // LANES
    table = jnp.asarray(fourier_rows(nphi, tiles).astype(np.float32))
    vmem = pl.BlockSpec(memory_space=pltpu.VMEM)
    whole = (tiles // 2, orders, 2 * channels * cycles)
    wigner = wigner.reshape(orders * channels * cycles // BLOCK, BLOCK, waves)
    operands = (
        values.reshape(rows, LANES),
        coords,
        cycle_ids.reshape(rows, LANES),
        pixels.reshape(rows, LANES),
        table,
        wigner,
        beam,
    )
    return pl.pallas_call(
        lambda *refs: deposit_kernel(blocks, cycles, nphi, nyquist, *refs),
        out_shape=[
            pltpu.VMEM(whole, jnp.bfloat16),
            pltpu.VMEM((RADIX // 2 + 1, 2 * whole[2], 2 * BLOCK), jnp.bfloat16),
            pltpu.VMEM(table.shape, jnp.float32),
            pltpu.VMEM(wigner.shape, wigner.dtype),
            pltpu.VMEM(beam.shape, beam.dtype),
        ],
        in_specs=[pl.BlockSpec(memory_space=pltpu.SMEM)]
        + [pl.BlockSpec(memory_space=pltpu.HBM)] * len(operands),
        out_specs=[vmem] * 5,
        scratch_shapes=[
            pltpu.VMEM((rows, LANES), jnp.float32),
            pltpu.VMEM(coords.shape, jnp.float32),
            pltpu.VMEM((rows, LANES), jnp.int32),
            pltpu.VMEM((rows, LANES), jnp.int32),
            pltpu.VMEM((7, rows, LANES), jnp.float32),
            pltpu.VMEM((channels * cycles * blocks, CHUNK), jnp.bfloat16),
            pltpu.VMEM((BLOCK, CHUNK), jnp.bfloat16),
            pltpu.VMEM((channels * cycles * blocks, BLOCK), jnp.float32),
            pltpu.VMEM(whole, jnp.float32),
            pltpu.SemaphoreType.DMA((len(operands),)),
        ],
        compiler_params=pltpu.CompilerParams(vmem_limit_bytes=40 * 2**20),
    )(place, *[pltpu.with_memory_space_constraint(x, pltpu.HBM) for x in operands])


def project_kernel(scale, parts_ref, wigner_ref, beam_ref, out_ref, sky, tall):
    orders, lanes = parts_ref.shape[1:]
    depth = lanes // 2
    pack = BLOCK // depth
    summed = jnp.sum(parts_ref[...].astype(jnp.float32), axis=0)
    share = orders // RADIX
    for m in range(RADIX):
        for x in range(2):
            tall[pl.ds(2 * m + x, share, stride=2 * RADIX), :] = summed[
                m * share : (m + 1) * share, x * depth : (x + 1) * depth
            ]
    row = lax.broadcasted_iota(jnp.int32, (2 * orders, BLOCK), 0)
    lane = lax.broadcasted_iota(jnp.int32, (2 * orders, BLOCK), 1)
    mine = (row >> 1 & pack - 1) == lane >> log2(depth)
    second = lane >> log2(depth // 2) & 1
    wide = jnp.where(mine, jnp.concatenate([tall[...]] * pack, axis=1), 0.0)
    tops = [
        jnp.where(second == c, part.astype(jnp.float32), 0.0) for part in split(wide) for c in range(2)
    ]
    beam = beam_ref[...] * scale
    height = 2 * pack
    for g in range(orders // pack):
        rows = slice(height * g, height * (g + 1))
        lhs = jnp.concatenate([top[rows] for top in tops], axis=0).astype(jnp.bfloat16)
        product = jnp.dot(lhs, wigner_ref[g], preferred_element_type=jnp.float32)
        first, other = (
            product[c * height : (c + 1) * height] + product[(c + 2) * height : (c + 3) * height]
            for c in range(2)
        )
        sky[rows, :] = first * beam[0:1] + other * beam[1:2]
    step = sky.shape[1] // out_ref.shape[0]
    over = step - LANES
    fold = LANES // over
    piece = sky.shape[0] // fold
    for k in range(out_ref.shape[0]):
        start = k * step
        rest = [
            sky[j * piece : (j + 1) * piece, start + LANES : start + step] for j in range(fold)
        ]
        out_ref[k] = jnp.concatenate(
            [sky[:, start : start + LANES], jnp.concatenate(rest, axis=1)], axis=0
        ).astype(jnp.bfloat16)


def partial_sky(parts, wigner, beam, groups, scale):
    orders, waves = parts.shape[1], beam.shape[1]
    vmem = pl.BlockSpec(memory_space=pltpu.VMEM)
    whole = (groups, 2 * orders * (waves // groups) // LANES, LANES)
    return pl.pallas_call(
        lambda *refs: project_kernel(scale, *refs),
        out_shape=jax.ShapeDtypeStruct(whole, jnp.bfloat16),
        in_specs=[vmem] * 3,
        out_specs=vmem,
        scratch_shapes=[
            pltpu.VMEM((2 * orders, waves), jnp.float32),
            pltpu.VMEM((2 * orders, parts.shape[2] // 2), jnp.float32),
        ],
        compiler_params=pltpu.CompilerParams(vmem_limit_bytes=16 * 2**20),
    )(parts, wigner, beam)


def finish_kernel(parts_ref, out_ref):
    total = jnp.sum(parts_ref[...].astype(jnp.float32), axis=0)
    orders, two, waves = out_ref.shape
    over = waves - LANES
    fold = LANES // over
    main, rest = total[: 2 * orders], total[2 * orders :]
    tail = jnp.concatenate([rest[:, j * over : (j + 1) * over] for j in range(fold)], axis=0)
    out_ref[...] = jnp.concatenate([main, tail], axis=1).reshape(orders, two, waves)


def finish(parts, orders, waves):
    vmem = pl.BlockSpec(memory_space=pltpu.VMEM)
    return pl.pallas_call(
        finish_kernel,
        out_shape=jax.ShapeDtypeStruct((orders, 2, waves), jnp.float32),
        in_specs=[vmem],
        out_specs=vmem,
        compiler_params=pltpu.CompilerParams(vmem_limit_bytes=2 * 2**20),
    )(parts)


def body(sample_values, sample_coords, tile_ids, phi_pixels, wigner_table, beam):
    tiles = lax.axis_size("theta")
    groups = lax.axis_size("psi")
    orders, channels, cycles, waves = wigner_table.shape
    nphi = 2 * tiles * orders
    nyquist = groups * channels // 2
    place = (2 * lax.axis_index("psi") + (lax.axis_index("theta") & 1)).astype(jnp.int32).reshape(1)
    samples = (sample_values, sample_coords, tile_ids, phi_pixels)
    other, operands, table, wigner, beam = partial_orders(
        place, *samples, wigner_table, beam, nphi, nyquist, tiles
    )
    arrived = lax.ppermute(other, "theta", [(i, i ^ 1) for i in range(tiles)])
    own = own_orders(place, table, operands, other.shape)
    freq = (own.astype(jnp.float32) + arrived.astype(jnp.float32)).astype(jnp.bfloat16)
    sides = [list(range(side, tiles, 2)) for side in range(2)]
    freq = lax.all_to_all(
        freq, "theta", split_axis=0, concat_axis=0, axis_index_groups=sides, tiled=True
    )
    sky = partial_sky(freq, wigner, beam, groups, 1.0 / math.sqrt(groups * channels))
    sky = lax.all_to_all(sky, "psi", split_axis=0, concat_axis=0, tiled=True)
    return jnp.moveaxis(finish(sky, orders, waves // groups), 1, 0)


def solution(mesh):
    in_specs = (
        P("theta"),
        P(None, "theta"),
        P("theta", None),
        P("theta"),
        P("theta", "psi", None, None),
        P("psi", None),
    )
    out_specs = P(None, "theta", "psi")
    return jax.shard_map(body, mesh=mesh, in_specs=in_specs, out_specs=out_specs, check_vma=False)
```
